128 devices in a mesh: grp: 8 (over x, core), blk: 16 (over y, z).
Axes of the slice: x: 4, y: 4, z: 4, core: 2. Of those that a mesh axis runs over, the one named last changes fastest.
Arguments:
- img_feats: bfloat16 [16384, 1024], P(('grp', 'blk')), may hold values from -8 to 8
- txt_feats: bfloat16 [16384, 1024], P(('grp', 'blk')), may hold values from -8 to 8
- img_head: bfloat16 [1024, 1024], replicated, may hold values from -1 to 1
- txt_head: bfloat16 [1024, 1024], replicated, may hold values from -1 to 1
- cluster_ids: int32 [16384, 1], P(('grp', 'blk')), may hold values from 0 to 127; in each aligned block of 128 rows (0 to 127, 128 to 255, ...) at most 2 rows name the same one
- placement: int32 [128], replicated, may hold values from 0 to 127, each once
- log_scale: float32 [1], replicated, may hold values from 2.3 to 2.9
- bias: float32 [1], replicated, may hold values from -6 to -3
Outputs:
- img_feat_grad: float32 [16384, 1024], P(('grp', 'blk'))
- txt_feat_grad: float32 [16384, 1024], P(('grp', 'blk'))
- pair_loss: float32 [16384], P(('grp', 'blk'))
The draws below stay inside these ranges and needn't reach their ends.
Inputs may be any that keep to these rules, and one draw needn't show every extreme that they name: `cluster_ids`: among the rows of one device at most 2 pairs name the same cluster, a bound that some block reaches of them; over all 16384 pairs every cluster is named by some pair. Each device index along grp+blk (grp slowest) appears once; the pairs of cluster c are gathered on the device of index placement[c], of team placement[c] // 16.
All inputs are finite; a program needn't handle non-finite values.
Results may differ from the reference program's by a relative error of at most 0.0025.
Values may be sent and summed in bfloat16 or wider, within the bound.
A program may use at most 128 MiB of HBM per device.

```python
import math
import jax
import jax.numpy as jnp
import numpy as np
from jax import lax

H = 1024
E = 1024
PAIRS_DEV = 128
CLUSTERS = 128
SLOT = 2
GROUP_ROWS = 4096
TOTAL = 16384
N_GRP = 8
N_BLK = 16


def draw_values(key, extent):
    normal_part = jax.random.normal(key, extent, jnp.float32)
    return normal_part


def pair_base(key):
    key = jax.random.fold_in(key, 101)
    streams = jax.random.split(key, 3)
    topics = draw_values(streams[0], (4, H))
    loadings = draw_values(streams[1], (TOTAL, 4))
    mixed = math.sqrt(0.2) * draw_values(streams[2], (TOTAL, H))
    for index in range(4):
        mixed = mixed + math.sqrt(0.1375) * loadings[:, index:index + 1] * topics[index][None, :]
    return mixed


def head_base(key):
    key = jax.random.fold_in(key, 202)
    return jax.random.normal(key, (H, E), jnp.float32)


def draw_img_feats(key, part):
    base = pair_base(key)
    key = jax.random.fold_in(key, 3)
    noise = draw_values(key, (TOTAL, H))
    return jnp.clip(base + 0.5 * noise, -8.0, 8.0).astype(jnp.bfloat16)


def draw_txt_feats(key, part):
    base = pair_base(key)
    key = jax.random.fold_in(key, 4)
    noise = draw_values(key, (TOTAL, H))
    return jnp.clip(base + 0.5 * noise, -8.0, 8.0).astype(jnp.bfloat16)


def draw_img_head(key, part):
    base = head_base(key)
    key = jax.random.fold_in(key, 5)
    single = jax.random.normal(key, (H, E), jnp.float32)
    return jnp.clip((base + 0.5 * single) / math.sqrt(1.25 * H), -1.0, 1.0).astype(jnp.bfloat16)


def draw_txt_head(key, part):
    base = head_base(key)
    key = jax.random.fold_in(key, 6)
    single = jax.random.normal(key, (H, E), jnp.float32)
    return jnp.clip((base + 0.5 * single) / math.sqrt(1.25 * H), -1.0, 1.0).astype(jnp.bfloat16)


def routed_block(own_key, own, number, rows, number_of, top, bound, skew):
    sequence = jax.random.permutation(own_key, number_of)
    crowded, usual = portions_of(number_of, rows * top, bound, skew, True), portions_of(number_of, rows * top, bound, skew, False)
    places = jnp.arange(number_of)

    def named(sizes, rotation):
        used = int((sizes > 0).sum())
        fixed = max(1, used // 4)
        moved = fixed + (places - fixed + rotation * (used - fixed)) % max(1, number_of - fixed)
        return jnp.zeros((number_of,), jnp.int32).at[sequence[jnp.where(places < fixed, places, moved)]].set(jnp.asarray(sizes, jnp.int32))

    sizes = jnp.where(number % 4 == 0, named(crowded, number // 4), named(usual, number - number // 4 - 1))
    mixed = jax.random.permutation(jax.random.fold_in(own, 3), number_of)
    donor, sink = mixed[0:number_of // 2 * 2:2], mixed[1:number_of // 2 * 2:2]
    room = jnp.minimum(sizes[donor] - 1, bound - sizes[sink]) // 2
    room = jnp.where((donor == sequence[0]) | (sink == sequence[0]) | (sizes[sink] == 0), 0, jnp.maximum(room, 0))
    moved = jax.random.randint(jax.random.fold_in(own, 4), (number_of // 2,), 0, 1 << 20) % (room + 1)
    sizes = sizes.at[donor].add(-moved).at[sink].add(moved)
    members = jnp.searchsorted(jnp.cumsum(sizes), jnp.arange(rows * top), side="right").astype(jnp.int32)
    listing = members.reshape(top, rows).T
    listing = listing[jax.random.permutation(jax.random.fold_in(own, 1), rows)]
    rotation = jax.random.randint(jax.random.fold_in(own, 2), (rows, 1), 0, top)
    return jnp.take_along_axis(listing, (jnp.arange(top)[None, :] + rotation) % top, axis=1)


def portions_of(number_of, total, reach, lean, full):
    portions = [(1 << 20) // math.isqrt(rank ** lean) + 1 for rank in range(1, number_of + 1)]
    largest = reach if full else min(reach, max(-(-total // number_of), total * portions[0] // sum(portions)))
    least = 1 if total - largest >= number_of - 1 else 0
    given, spare = [largest] + [least] * (number_of - 1), total - largest - least * (number_of - 1)
    while spare > 0:
        candidates = [i for i in range(1, number_of) if given[i] < largest] or [i for i in range(1, number_of) if given[i] < reach]
        pool, budget = sum([portions[i] for i in candidates]), spare
        for i in candidates:
            extra = min(reach - given[i], max(1, budget * portions[i] // pool), spare)
            given[i] = given[i] + extra
            spare = spare - extra
    return np.array(given)


def setup_inputs(seed: int = 0) -> dict:
    arg_keys = jax.random.split(jax.random.key(seed), 9)
    img_feats = draw_img_feats(jax.random.fold_in(arg_keys[8], 71), 0)
    txt_feats = draw_txt_feats(jax.random.fold_in(arg_keys[8], 71), 0)
    img_head = draw_img_head(jax.random.fold_in(arg_keys[8], 71), 0)
    txt_head = draw_txt_head(jax.random.fold_in(arg_keys[8], 71), 0)
    cluster_ids_keys = jax.random.split(jax.random.fold_in(arg_keys[4], 1), TOTAL // PAIRS_DEV)
    cluster_ids_turns = jax.random.permutation(jax.random.fold_in(arg_keys[4], 3), TOTAL // PAIRS_DEV)
    cluster_ids = jax.vmap(lambda own, number: routed_block(jax.random.fold_in(arg_keys[4], 2), own, number, PAIRS_DEV, CLUSTERS, 1, SLOT, 2))(cluster_ids_keys, cluster_ids_turns).reshape((TOTAL, 1))
    placement = jax.random.permutation(arg_keys[5], CLUSTERS).astype(jnp.int32)
    log_scale = jnp.clip(jax.random.uniform(arg_keys[6], (1,), jnp.float32, 2.3, 2.9), 2.3, 2.9)
    bias = jnp.clip(jax.random.uniform(arg_keys[7], (1,), jnp.float32, -6.0, -3.0), -6.0, -3.0)
    return dict(img_feats=img_feats, txt_feats=txt_feats, img_head=img_head, txt_head=txt_head, cluster_ids=cluster_ids, placement=placement, log_scale=log_scale, bias=bias)


EPS = 1e-06

def unit_rows(feats, head):
    raw = jnp.dot(feats, head, preferred_element_type=jnp.float32)
    factor = lax.rsqrt(lax.optimization_barrier(jnp.sum(raw * raw, axis=1, keepdims=True)) + EPS)
    return (raw * factor, factor)

def tile_terms(images, image_live, texts, text_live, row_start, col_start, scale_t, shift):
    sims = lax.dot_general(images, texts, (((1,), (1,)), ((), ())), preferred_element_type=jnp.float32)
    logits = scale_t * sims + shift
    row_ids = row_start + jnp.arange(images.shape[0], dtype=jnp.int32)
    col_ids = col_start + jnp.arange(texts.shape[0], dtype=jnp.int32)
    sign = jnp.where(row_ids[:, None] == col_ids[None, :], 1.0, -1.0).astype(jnp.float32)
    live = image_live.astype(jnp.float32)[:, None] * text_live.astype(jnp.float32)[None, :]
    losses = -jax.nn.log_sigmoid(sign * logits) * live
    weights = (scale_t * -sign * jax.nn.sigmoid(-sign * logits) * live).astype(jnp.bfloat16)
    return (weights, lax.optimization_barrier(jnp.sum(losses, axis=1)))

def unit_backward(grad, unit, factor, head):
    along = lax.optimization_barrier(jnp.sum(unit * grad, axis=1, keepdims=True))
    local = ((grad - unit * along) * factor).astype(jnp.bfloat16)
    return lax.dot_general(local, head, (((1,), (1,)), ((), ())), preferred_element_type=jnp.float32)

def reference(img_feats, txt_feats, img_head, txt_head, cluster_ids, placement, log_scale, bias):
    img_unit, img_factor = unit_rows(img_feats, img_head)
    txt_unit, txt_factor = unit_rows(txt_feats, txt_head)
    img_emb = img_unit.astype(jnp.bfloat16)
    txt_emb = txt_unit.astype(jnp.bfloat16)
    target = jnp.take(placement, cluster_ids[:, 0], axis=0).astype(jnp.int32)
    team = target // N_BLK
    scale_t = jnp.exp(log_scale[0])
    shift = bias[0]
    total = img_feats.shape[0]
    width = img_head.shape[1]
    capacity = min(GROUP_ROWS, total)

    def per_team(index):
        away = (team != index).astype(jnp.int32)
        order = jnp.argsort(away, stable=True)[:capacity].astype(jnp.int32)
        count = jnp.sum(1 - away)
        live = (jnp.arange(capacity, dtype=jnp.int32) < count).astype(jnp.float32)
        images = jnp.take(img_emb, order, axis=0)
        texts = jnp.take(txt_emb, order, axis=0)
        weights, losses = tile_terms(images, live, texts, live, 0, 0, scale_t, shift)
        img_grad = jnp.dot(weights, texts, preferred_element_type=jnp.float32)
        txt_grad = lax.dot_general(weights, images, (((0,), (0,)), ((), ())), preferred_element_type=jnp.float32)
        return (order, img_grad, txt_grad, losses)
    orders, img_grads, txt_grads, losses = lax.map(per_team, jnp.arange(N_GRP, dtype=jnp.int32))
    flat_order = orders.reshape(-1)
    emb_grad_img = jnp.zeros((total, width), jnp.float32).at[flat_order].add(img_grads.reshape(-1, width))
    emb_grad_txt = jnp.zeros((total, width), jnp.float32).at[flat_order].add(txt_grads.reshape(-1, width))
    pair_loss = jnp.zeros((total,), jnp.float32).at[flat_order].add(losses.reshape(-1)) / (N_BLK * PAIRS_DEV)
    img_feat_grad = unit_backward(emb_grad_img, img_unit, img_factor, img_head)
    txt_feat_grad = unit_backward(emb_grad_txt, txt_unit, txt_factor, txt_head)
    return (img_feat_grad, txt_feat_grad, pair_loss)
```

```python
import functools

import jax
import jax.numpy as jnp
from jax import lax
from jax.experimental import pallas as pl
from jax.experimental.pallas import tpu as pltpu
from jax.sharding import PartitionSpec as P

EPS = 1e-06
CORES = 2
RING = 4
PEERS = 8
SLOTS = 32
HALF = SLOTS // 2
BLOCK = PEERS * SLOTS
EXTRA = 128
LEVELS = 32000.0
MESH = pl.DeviceIdType.MESH
F32 = jnp.float32
BF16 = jnp.bfloat16


def dot(a, b, da, db):
    return lax.dot_general(a, b, (((da,), (db,)), ((), ())), preferred_element_type=F32)


def encode(values, loss):
    rows = values.shape[0]
    top = jnp.max(jnp.abs(values), axis=1, keepdims=True)
    grade = jnp.ceil(8.0 * jnp.log2(jnp.maximum(top, 1e-30)))
    steps = jnp.round(values * (LEVELS * jnp.exp2(-0.125 * grade)))
    lane = lax.broadcasted_iota(jnp.int32, (rows, EXTRA), 1)
    extra = jnp.where(lane == 0, grade, 0.0)
    if loss is not None:
        loss_grade = jnp.ceil(8.0 * jnp.log2(jnp.maximum(loss, 1e-30)))
        scaled = loss * (LEVELS * jnp.exp2(-0.125 * loss_grade))
        high = jnp.round(scaled)
        low = jnp.round((scaled - high) * LEVELS)
        extra = jnp.where(lane == 1, loss_grade, extra)
        extra = jnp.where(lane == 2, high, extra)
        extra = jnp.where(lane == 3, low, extra)
    return steps.astype(jnp.int32).astype(jnp.int16), extra.astype(jnp.int32).astype(jnp.int16)


def decode(steps, extra, with_loss):
    values = steps * (jnp.exp2(0.125 * extra[:, 0:1]) * (1.0 / LEVELS))
    if not with_loss:
        return values, None
    scale = jnp.exp2(0.125 * extra[:, 1:2]) * (1.0 / LEVELS)
    return values, (extra[:, 2:3] + extra[:, 3:4] * (1.0 / LEVELS)) * scale


def kernel(
    scale_ref,
    bias_ref,
    img_feats,
    txt_feats,
    img_head,
    txt_head,
    ids,
    placement,
    out_img,
    out_txt,
    out_loss,
    layout,
    unit,
    factor,
    pack,
    held,
    live,
    coef,
    losses,
    part,
    away,
    near,
    far,
    back,
    sa,
    ra,
    sg,
    rg,
    sl,
    rl,
    s1,
    r1,
    s2,
    r2,
    sb,
    rb,
):
    width = img_head.shape[1]
    pairs = img_feats.shape[0]
    g = lax.axis_index("grp")
    b = lax.axis_index("blk")
    x, core = lax.div(g, CORES), lax.rem(g, CORES)
    y, z = lax.div(b, RING), lax.rem(b, RING)

    def peer(k):
        dx, dc = lax.div(k, CORES), lax.rem(k, CORES)
        return (lax.rem(x + dx, RING) * CORES + lax.rem(core + dc, CORES), b)

    def facing(k):
        dx, dc = lax.div(k, CORES), lax.rem(k, CORES)
        return lax.rem(RING - dx, RING) * CORES + dc

    def neighbour(kind, side):
        step = 1 if side == 0 else RING - 1
        if kind == 0:
            return (g, y * RING + lax.rem(z + step, RING))
        return (g, lax.rem(y + step, RING) * RING + z)

    def copy(src, dst, send, recv, device):
        return pltpu.make_async_remote_copy(
            src_ref=src,
            dst_ref=dst,
            send_sem=send,
            recv_sem=recv,
            device_id=device,
            device_id_type=MESH,
        )

    def chunk(k):
        return pl.ds(pl.multiple_of(k * SLOTS, SLOTS), SLOTS)

    barrier = pltpu.get_barrier_semaphore()

    @pl.loop(1, PEERS)
    def _(k):
        pl.semaphore_signal(barrier, inc=1, device_id=peer(k), device_id_type=MESH)

    for kind in range(2):
        for side in range(2):
            pl.semaphore_signal(
                barrier, inc=1, device_id=neighbour(kind, side), device_id_type=MESH
            )

    lane = lax.broadcasted_iota(jnp.int32, (pairs, 128), 1)
    row = lax.broadcasted_iota(jnp.int32, (pairs, 128), 0)
    place = placement[...].astype(F32)
    target = jnp.sum(jnp.where(ids[...] == lane, place, 0.0), axis=1, keepdims=True)
    team = jnp.floor(target * (1.0 / (RING * RING)))
    team_x = jnp.floor(team * (1.0 / CORES))
    dx = team_x - x.astype(F32)
    dc = team - CORES * team_x - core.astype(F32)
    where_to = CORES * jnp.where(dx < 0, dx + RING, dx) + jnp.where(dc < 0, dc + CORES, dc)
    chosen = jnp.where(where_to == lane.astype(F32), 1.0, 0.0)
    before = jnp.where(row > lane, 1.0, 0.0).astype(BF16)
    earlier = dot(before, chosen.astype(BF16), 1, 0)
    rank = jnp.sum(earlier * chosen, axis=1, keepdims=True)
    slot = where_to * SLOTS + rank
    slots = lax.broadcasted_iota(jnp.int32, (pairs, BLOCK), 1).astype(F32)
    layout[...] = jnp.where(slots == slot, 1.0, 0.0).astype(BF16)

    filled = dot(layout[...], jnp.ones((pairs, 128), BF16), 0, 0)
    lane_block = lax.broadcasted_iota(jnp.int32, (BLOCK, 128), 1)
    mark = jnp.where(lane_block == 0, 2.0 - 2.0 * filled, 0.0)

    pl.semaphore_wait(barrier, PEERS - 1 + 4)

    for kind, feats, head in ((0, img_feats, img_head), (1, txt_feats, txt_head)):
        raw = dot(feats[...], head[...], 1, 0)
        scale_back = lax.rsqrt(jnp.sum(raw * raw, axis=1, keepdims=True) + EPS)
        unit[kind] = raw * scale_back
        factor[kind] = jnp.broadcast_to(scale_back, (pairs, 128))
        rows = dot(layout[...], unit[kind].astype(BF16), 0, 0)
        pack[kind, :, 128:] = rows[:, 128:].astype(BF16)
        pack[kind, :, :128] = (rows[:, :128] + mark).astype(BF16)

        @pl.loop(1, PEERS)
        def _(k):
            copy(
                pack.at[kind, chunk(k)],
                held.at[kind, 0, chunk(facing(k))],
                sa.at[kind, k],
                ra.at[kind, facing(k)],
                peer(k),
            ).start()

        held[kind, 0, :SLOTS] = pack[kind, :SLOTS]

    def gathered(kind, side, k):
        return copy(
            held.at[kind, 0, chunk(k)],
            held.at[kind, 3 if side == 0 else 1, chunk(k)],
            sg.at[kind, side, k],
            rg.at[kind, side, k],
            neighbour(kind, side),
        )

    def passed(kind, side, k):
        rows = pl.ds(pl.multiple_of(k * SLOTS + side * HALF, HALF), HALF)
        return copy(
            held.at[kind, 3 if side == 0 else 1, rows],
            held.at[kind, 2, rows],
            sl.at[kind, side, k],
            rl.at[kind, side, k],
            neighbour(kind, side),
        )

    def arrived(kind, k):
        return copy(
            pack.at[kind, chunk(k)],
            held.at[kind, 0, chunk(k)],
            sa.at[kind, k],
            ra.at[kind, k],
            peer(k),
        )

    for kind in range(2):
        for side in range(2):
            gathered(kind, side, 0).start()

    @pl.loop(1, PEERS)
    def _(k):
        for kind in range(2):
            arrived(kind, k).wait_recv()
            for side in range(2):
                gathered(kind, side, k).start()

    @pl.loop(0, PEERS)
    def _(k):
        for kind in range(2):
            for side in range(2):
                gathered(kind, side, k).wait_recv()
                passed(kind, side, k).start()

    @pl.loop(0, PEERS)
    def _(k):
        for kind in range(2):
            for side in range(2):
                passed(kind, side, k).wait_recv()

    scale_t = jnp.exp(jnp.full((1, BLOCK), scale_ref[0], F32))
    shift = bias_ref[0]
    first_lane = jnp.where(lax.broadcasted_iota(jnp.int32, (8, 128), 1) == 0, 1.0, 0.0)
    for j in range(RING):
        heads_of = dot(first_lane.astype(BF16), held[1, j, :, :128], 1, 1)
        live[j] = jnp.where(heads_of < 1.5, 1.0, 0.0)
    losses[...] = jnp.zeros_like(losses)
    same = lax.broadcasted_iota(jnp.int32, (BLOCK, BLOCK), 0) == lax.broadcasted_iota(
        jnp.int32, (BLOCK, BLOCK), 1
    )

    @pl.loop(0, RING * RING)
    def _(t):
        i, j = lax.div(t, RING), lax.rem(t, RING)
        images = held[0, i]
        sims = dot(images, held[1, j], 1, 1)
        own = jnp.where(t == 0, 1.0, 0.0)
        sign = jnp.where(same, 1.0 - 2.0 * own, 1.0)
        logits = sign * (scale_t * sims + shift)
        small = jnp.exp(-jnp.abs(logits))
        whole = 1.0 + small
        inverse = 1.0 / whole
        image_live = jnp.where(images[:, 0:1].astype(F32) < 1.5, 1.0, 0.0)
        text_live = live[j][0:1]
        log_term = jnp.log(whole) + (small - (whole - 1.0)) * inverse
        terms = (jnp.maximum(logits, 0.0) + log_term) * text_live
        losses[i] += terms[:, :128] + terms[:, 128:]
        rate = jnp.where(logits >= 0, inverse, small * inverse)
        weights = (sign * scale_t) * rate * (image_live * text_live)
        coef[
            pl.ds(pl.multiple_of(i * BLOCK, BLOCK), BLOCK),
            pl.ds(pl.multiple_of(j * BLOCK, BLOCK), BLOCK),
        ] = weights.astype(BF16)

    def terms_of(kind, n):
        @pl.loop(0, width // 256)
        def _(q):
            lanes = pl.ds(pl.multiple_of(q * 256, 256), 256)
            total = jnp.zeros((BLOCK, 256), F32)
            for j in range(RING):
                if kind == 0:
                    total += dot(
                        coef[n * BLOCK : (n + 1) * BLOCK, j * BLOCK : (j + 1) * BLOCK],
                        held[1, j, :, lanes],
                        1,
                        0,
                    )
                else:
                    total += dot(
                        coef[j * BLOCK : (j + 1) * BLOCK, n * BLOCK : (n + 1) * BLOCK],
                        held[0, j, :, lanes],
                        0,
                        0,
                    )
            part[kind, n, :, lanes] = total

    def loss_of(n, k):
        return jnp.sum(losses[n, chunk(k)], axis=1, keepdims=True)

    def store(kind, n, k, values, loss):
        steps, extra = encode(values, loss)
        away[kind, n, chunk(k), :width] = steps
        away[kind, n, chunk(k), width:] = extra

    def load(ref):
        value = ref[...].astype(F32)
        return value[:, :width], value[:, width:]

    def first(kind, side, k):
        rows = pl.ds(pl.multiple_of(k * SLOTS + side * HALF, HALF), HALF)
        return copy(
            away.at[kind, 2, rows],
            far.at[kind, side, k],
            s1.at[kind, side, k],
            r1.at[kind, side, k],
            neighbour(kind, side),
        )

    def second(kind, side, k):
        return copy(
            away.at[kind, 1 if side == 0 else 3, chunk(k)],
            near.at[kind, side, chunk(k)],
            s2.at[kind, side, k],
            r2.at[kind, side, k],
            neighbour(kind, side),
        )

    def last(kind, k):
        return copy(
            away.at[kind, 0, chunk(k)],
            back.at[kind, chunk(facing(k))],
            sb.at[kind, k],
            rb.at[kind, facing(k)],
            peer(k),
        )

    def returned(kind, k):
        return copy(
            away.at[kind, 0, chunk(k)],
            back.at[kind, chunk(k)],
            sb.at[kind, k],
            rb.at[kind, k],
            peer(k),
        )

    for kind in range(2):
        terms_of(kind, 2)

        @pl.loop(0, PEERS)
        def _(k):
            store(kind, 2, k, part[kind, 2, chunk(k)], loss_of(2, k) if kind == 0 else None)
            first(kind, 0, k).start()
            first(kind, 1, k).start()

    for kind in range(2):
        for n in (1, 3, 0):
            terms_of(kind, n)

    for kind in range(2):
        for side in range(2):
            n = 1 if side == 0 else 3

            @pl.loop(0, PEERS)
            def _(k):
                first(kind, side, k).wait_recv()
                steps, extra = load(far.at[kind, side, k])
                values, loss = decode(steps, extra, kind == 0)
                mine = part[kind, n, chunk(k)]
                pad = jnp.zeros((HALF, width), F32)
                order = [values, pad] if side == 0 else [pad, values]
                mine += jnp.concatenate(order, axis=0)
                loss_mine = None
                if kind == 0:
                    pad = jnp.zeros((HALF, 1), F32)
                    order = [loss, pad] if side == 0 else [pad, loss]
                    loss_mine = loss_of(n, k) + jnp.concatenate(order, axis=0)
                store(kind, n, k, mine, loss_mine)
                second(kind, side, k).start()

    for kind in range(2):

        def finish(k):
            mine = part[kind, 0, chunk(k)]
            loss_mine = loss_of(0, k) if kind == 0 else None
            for side in range(2):
                second(kind, side, k).wait_recv()
                steps, extra = load(near.at[kind, side, chunk(k)])
                values, loss = decode(steps, extra, kind == 0)
                mine += values
                if kind == 0:
                    loss_mine += loss
            store(kind, 0, k, mine, loss_mine)

        @pl.loop(1, PEERS)
        def _(k):
            finish(k)
            last(kind, k).start()

        finish(0)
        back[kind, :SLOTS] = away[kind, 0, :SLOTS]

    for kind, head, out in ((0, img_head, out_img), (1, txt_head, out_txt)):

        @pl.loop(1, PEERS)
        def _(k):
            returned(kind, k).wait_recv()

        steps = back[kind].astype(jnp.int32)
        high = lax.shift_right_arithmetic(steps, 8)
        low = steps - lax.shift_left(high, 8)
        high = dot(layout[...], high.astype(F32).astype(BF16), 1, 0)
        low = dot(layout[...], low.astype(F32).astype(BF16), 1, 0)
        own = high * 256.0 + low
        grad, loss = decode(own[:, :width], own[:, width:], kind == 0)
        if kind == 0:
            loss = jnp.broadcast_to(loss * (1.0 / (RING * RING * pairs)), (pairs, 128))
            out_loss[...] = jnp.transpose(loss)[0:8]
        along = jnp.sum(unit[kind] * grad, axis=1, keepdims=True)
        local = ((grad - unit[kind] * along) * factor[kind][:, 0:1]).astype(BF16)
        out[...] = dot(local, head[...], 1, 1)

    @pl.loop(1, PEERS)
    def _(k):
        for kind in range(2):
            arrived(kind, k).wait_send()
            last(kind, k).wait_send()

    @pl.loop(0, PEERS)
    def _(k):
        for kind in range(2):
            for side in range(2):
                gathered(kind, side, k).wait_send()
                passed(kind, side, k).wait_send()
                first(kind, side, k).wait_send()
                second(kind, side, k).wait_send()


def body(img_feats, txt_feats, img_head, txt_head, cluster_ids, placement, log_scale, bias):
    pairs, width = img_feats.shape[0], img_head.shape[1]
    wide = width + EXTRA
    dma = pltpu.SemaphoreType.DMA
    vmem, smem = pl.BlockSpec(memory_space=pltpu.VMEM), pl.BlockSpec(memory_space=pltpu.SMEM)
    img, txt, loss = pl.pallas_call(
        kernel,
        out_shape=(
            jax.ShapeDtypeStruct((pairs, width), F32),
            jax.ShapeDtypeStruct((pairs, width), F32),
            jax.ShapeDtypeStruct((8, pairs), F32),
        ),
        in_specs=[smem, smem] + [vmem] * 6,
        out_specs=(vmem, vmem, vmem),
        scratch_shapes=[
            pltpu.VMEM((pairs, BLOCK), BF16),
            pltpu.VMEM((2, pairs, width), F32),
            pltpu.VMEM((2, pairs, 128), F32),
            pltpu.VMEM((2, BLOCK, width), BF16),
            pltpu.VMEM((2, RING, BLOCK, width), BF16),
            pltpu.VMEM((RING, 8, BLOCK), F32),
            pltpu.VMEM((RING * BLOCK, RING * BLOCK), BF16),
            pltpu.VMEM((RING, BLOCK, 128), F32),
            pltpu.VMEM((2, RING, BLOCK, width), F32),
            pltpu.VMEM((2, RING, BLOCK, wide), jnp.int16),
            pltpu.VMEM((2, 2, BLOCK, wide), jnp.int16),
            pltpu.VMEM((2, 2, PEERS, HALF, wide), jnp.int16),
            pltpu.VMEM((2, BLOCK, wide), jnp.int16),
            dma((2, PEERS)),
            dma((2, PEERS)),
            dma((2, 2, PEERS)),
            dma((2, 2, PEERS)),
            dma((2, 2, PEERS)),
            dma((2, 2, PEERS)),
            dma((2, 2, PEERS)),
            dma((2, 2, PEERS)),
            dma((2, 2, PEERS)),
            dma((2, 2, PEERS)),
            dma((2, PEERS)),
            dma((2, PEERS)),
        ],
        compiler_params=pltpu.CompilerParams(
            collective_id=0, has_side_effects=True, vmem_limit_bytes=56 * 1024 * 1024
        ),
    )(
        log_scale,
        bias,
        img_feats,
        txt_feats,
        img_head,
        txt_head,
        cluster_ids,
        placement.reshape(1, -1),
    )
    return img, txt, loss[0]


def solution(mesh):
    placed = (
        P(("grp", "blk"), None),
        P(("grp", "blk"), None),
        P(),
        P(),
        P(("grp", "blk"), None),
        P(),
        P(),
        P(),
    )
    return jax.shard_map(
        body,
        mesh=mesh,
        in_specs=placed,
        out_specs=(P(("grp", "blk"), None), P(("grp", "blk"), None), P(("grp", "blk"))),
        check_vma=False,
    )
```

```python
import functools

import jax
import jax.numpy as jnp
from jax import lax
from jax.experimental import pallas as pl
from jax.experimental.pallas import tpu as pltpu
from jax.sharding import PartitionSpec as P

EPS = 1e-06
CORES = 2
RING = 4
PEERS = 8
MOST = 32
TILE = 256
EXTRA = 128
LEVELS = 32000.0
AROUND = (0, 1, 3, 2)
FACING = (0, 2, 1, 3)
OWN, NEXT, PREV, FAR = range(4)
MESH = pl.DeviceIdType.MESH
F32 = jnp.float32
BF16 = jnp.bfloat16
LOG2E = 1.4426950408889634


def dot(a, b, da, db):
    return lax.dot_general(a, b, (((da,), (db,)), ((), ())), preferred_element_type=F32)


def encode(values, loss, alarm):
    rows = values.shape[0]
    top = jnp.max(jnp.abs(values), axis=1, keepdims=True)
    grade = jnp.ceil(8.0 * jnp.log2(jnp.maximum(top, 1e-30)))
    steps = jnp.round(values * (LEVELS * jnp.exp2(-0.125 * grade)))
    lane = lax.broadcasted_iota(jnp.int32, (rows, EXTRA), 1)
    extra = jnp.where(lane == 0, grade, 0.0)
    if loss is not None:
        loss_grade = jnp.ceil(8.0 * jnp.log2(jnp.maximum(loss, 1e-30)))
        scaled = loss * (LEVELS * jnp.exp2(-0.125 * loss_grade))
        high = jnp.round(scaled)
        low = jnp.round((scaled - high) * LEVELS)
        extra = jnp.where(lane == 1, loss_grade, extra)
        extra = jnp.where(lane == 2, high, extra)
        extra = jnp.where(lane == 3, low, extra)
        extra = jnp.where(lane == 4, alarm, extra)
    return steps, extra


def decode(coded, width, with_loss):
    extra = coded[:, width:]
    values = coded[:, :width] * (jnp.exp2(0.125 * extra[:, 0:1]) * (1.0 / LEVELS))
    if not with_loss:
        return values, None, None
    scale = jnp.exp2(0.125 * extra[:, 1:2]) * (1.0 / LEVELS)
    loss = (extra[:, 2:3] + extra[:, 3:4] * (1.0 / LEVELS)) * scale
    return values, loss, extra[:, 4:5]


def kernel(
    slots,
    scale_ref,
    bias_ref,
    img_feats,
    txt_feats,
    img_head,
    txt_head,
    ids,
    placement,
    out_img,
    out_txt,
    out_loss,
    out_alarm,
    feats,
    head,
    layout,
    unit,
    factor,
    pack,
    held,
    coef,
    turned,
    losses,
    part,
    away,
    near,
    far,
    back,
    si,
    sa,
    ra,
    sg,
    rg,
    sl,
    rl,
    s1,
    r1,
    s2,
    r2,
    sb,
    rb,
):
    width = img_head.shape[1]
    pairs = img_feats.shape[0]
    groups = slots // 8
    block = PEERS * groups
    block_rows = PEERS * slots
    early = 3 * block_rows // TILE
    g = lax.axis_index("grp")
    b = lax.axis_index("blk")
    x, core = lax.div(g, CORES), lax.rem(g, CORES)
    y, z = lax.div(b, RING), lax.rem(b, RING)

    def peer(k):
        to_x = lax.rem(x + AROUND[k // CORES], RING)
        return (to_x * CORES + lax.rem(core + k % CORES, CORES), b)

    def facing(k):
        return FACING[k // CORES] * CORES + k % CORES

    def neighbour(kind, side):
        step = 1 if side == 0 else RING - 1
        if kind == 0:
            return (g, y * RING + lax.rem(z + step, RING))
        return (g, lax.rem(y + step, RING) * RING + z)

    def copy(src, dst, send, recv, device):
        return pltpu.make_async_remote_copy(
            src_ref=src,
            dst_ref=dst,
            send_sem=send,
            recv_sem=recv,
            device_id=device,
            device_id_type=MESH,
        )

    def chunk(k, at=0):
        return pl.ds(at * block + k * groups, groups)

    loads = []
    for n, (src, dst) in enumerate(
        (
            (img_feats, feats.at[0]),
            (img_head, head.at[0]),
            (txt_feats, feats.at[1]),
            (txt_head, head.at[1]),
        )
    ):
        loads.append(pltpu.make_async_copy(src, dst, si.at[n]))
        loads[-1].start()

    barrier = pltpu.get_barrier_semaphore()
    for k in range(1, PEERS):
        pl.semaphore_signal(barrier, inc=1, device_id=peer(k), device_id_type=MESH)
    for kind in range(2):
        for side in range(2):
            pl.semaphore_signal(
                barrier, inc=1, device_id=neighbour(kind, side), device_id_type=MESH
            )

    lane = lax.broadcasted_iota(jnp.int32, (pairs, 128), 1)
    row = lax.broadcasted_iota(jnp.int32, (pairs, 128), 0)
    lane_f = lane.astype(F32)
    place = placement[...].astype(F32)
    named = jnp.transpose(jnp.broadcast_to(ids[...].astype(F32), (pairs, pairs)))
    target = jnp.sum(jnp.where(named == lane_f, place, 0.0), axis=1, keepdims=True)
    team = jnp.floor(target * (1.0 / (RING * RING)))
    team_x = jnp.floor(team * (1.0 / CORES))
    dx = team_x - x.astype(F32)
    dx = jnp.where(dx < 0, dx + RING, dx)
    dx = jnp.where(dx == 2, 3.0, jnp.where(dx == 3, 2.0, dx))
    dc = team - CORES * team_x - core.astype(F32)
    where_to = CORES * dx + jnp.where(dc < 0, dc + CORES, dc)
    chosen = jnp.where(where_to == lane_f, 1.0, 0.0)
    before = jnp.where(row > lane, 1.0, 0.0).astype(BF16)
    earlier = dot(before, chosen.astype(BF16), 1, 0)
    rank = jnp.sum(earlier * chosen, axis=1, keepdims=True)
    slot = jnp.where(rank < slots, where_to * slots + rank, -1.0)
    spots = lax.broadcasted_iota(jnp.int32, (pairs, TILE), 1).astype(F32)
    layout[...] = jnp.where(spots == slot, 1.0, 0.0).astype(BF16)

    crowded = jnp.where(jnp.max(rank, axis=0, keepdims=True) >= slots, 4.0, 0.0)
    filled = dot(layout[...], jnp.ones((pairs, 128), BF16), 0, 0)[:block_rows]
    lane_block = lax.broadcasted_iota(jnp.int32, (block_rows, 128), 1)
    row_block = lax.broadcasted_iota(jnp.int32, (block_rows, 128), 0)
    mark = 2.0 - 2.0 * filled
    if slots < MOST:
        mark += jnp.where(lax.rem(row_block, slots) == 0, crowded, 0.0)
    mark = jnp.where(lane_block == 0, mark, 0.0)

    def arrived(kind, k):
        return copy(
            pack.at[kind, chunk(k)],
            held.at[kind, chunk(k)],
            sa.at[kind, k],
            ra.at[kind, k],
            peer(k),
        )

    def gathered(kind, side, k):
        return copy(
            held.at[kind, chunk(k)],
            held.at[kind, chunk(k, PREV if side == 0 else NEXT)],
            sg.at[kind, side, k],
            rg.at[kind, side, k],
            neighbour(kind, side),
        )

    def passed(kind, k):
        side = k % 2
        return copy(
            held.at[kind, chunk(k, PREV if side == 0 else NEXT)],
            held.at[kind, chunk(k, FAR)],
            sl.at[kind, k],
            rl.at[kind, k],
            neighbour(kind, side),
        )

    for kind in range(2):
        loads[2 * kind].wait()
        loads[2 * kind + 1].wait()
        raw = dot(feats[kind], head[kind], 1, 0)
        scale_back = lax.rsqrt(jnp.sum(raw * raw, axis=1, keepdims=True) + EPS)
        unit[kind] = raw * scale_back
        factor[kind] = jnp.broadcast_to(scale_back, (pairs, 128))
        rows = dot(layout[...], unit[kind].astype(BF16), 0, 0)[:block_rows]
        first = (rows[:, :128] + mark).reshape(block, 8, 128)
        pack[kind, :, :, :128] = first.astype(BF16)
        pack[kind, :, :, 128:] = rows[:, 128:].reshape(block, 8, width - 128).astype(BF16)
        held[kind, :groups] = pack[kind, :groups]
        if kind == 0:
            pl.semaphore_wait(barrier, PEERS - 1 + 4)
        for k in range(1, PEERS):
            copy(
                pack.at[kind, chunk(k)],
                held.at[kind, chunk(facing(k))],
                sa.at[kind, k],
                ra.at[kind, facing(k)],
                peer(k),
            ).start()
        for side in range(2):
            gathered(kind, side, 0).start()

    def pass_on(k):
        for kind in range(2):
            gathered(kind, k % 2, k).wait_recv()
            passed(kind, k).start()

    for k in range(1, PEERS):
        for kind in range(2):
            arrived(kind, k).wait_recv()
            for side in range(2):
                gathered(kind, side, k).start()
        pass_on(k - 1)
    pass_on(PEERS - 1)
    for k in range(PEERS):
        for kind in range(2):
            gathered(kind, 1 - k % 2, k).wait_recv()

    scale_t = jnp.exp(jnp.full((1, 1), scale_ref[0], F32))
    shift = bias_ref[0]
    first_lane = jnp.where(lax.broadcasted_iota(jnp.int32, (8, 128), 1) == 0, 1.0, 0.0)
    losses[...] = jnp.zeros_like(losses)

    def tile_of(i, j, with_own):
        span = TILE // 8
        images = held[0, pl.ds(i * span, span)].reshape(TILE, width)
        texts = held[1, pl.ds(j * span, span)].reshape(TILE, width)
        sims = dot(images, texts, 1, 1)
        text_first = dot(first_lane.astype(BF16), texts[:, :128], 1, 1)[0:1]
        base = jnp.where(text_first < 1.5, shift * LOG2E, -1e5)
        powers = sims * (scale_t * LOG2E) + base
        if with_own:
            row = lax.broadcasted_iota(jnp.int32, (TILE, TILE), 0)
            same = row == lax.broadcasted_iota(jnp.int32, (TILE, TILE), 1)
            same = jnp.logical_and(same, row < block_rows)
            same = jnp.logical_and(same, powers > -5e4)
            powers = jnp.where(same, -powers, powers)
        odds = jnp.exp2(powers)
        whole = 1.0 + odds
        inverse = 1.0 / whole
        terms = jnp.log(whole) + (odds - (whole - 1.0)) * inverse
        rows = pl.ds(pl.multiple_of(i * TILE, TILE), TILE)
        columns = pl.ds(pl.multiple_of(j * TILE, TILE), TILE)
        losses[rows] += terms[:, :128] + terms[:, 128:]
        weights = odds * inverse * jnp.where(images[:, 0:1].astype(F32) < 1.5, scale_t, 0.0)
        if with_own:
            weights = jnp.where(same, -weights, weights)
        coef[rows, columns] = weights.astype(BF16)
        turned[columns, rows] = jnp.transpose(weights).astype(BF16)

    tile_of(0, 0, True)

    @pl.loop(1, early * early)
    def _(t):
        tile_of(lax.div(t, early), lax.rem(t, early), False)

    for k in range(PEERS):
        for kind in range(2):
            passed(kind, k).wait_recv()

    @pl.loop(0, early)
    def _(t):
        tile_of(t, early, False)

    @pl.loop(0, early + 1)
    def _(t):
        tile_of(early, t, False)

    alarm = None
    if slots < MOST:
        starts = jnp.zeros((8, 128), F32)
        for kind in range(2):
            starts = jnp.maximum(starts, jnp.max(held[kind, :, :, :128].astype(F32), axis=0))
        starts = jnp.where(lax.broadcasted_iota(jnp.int32, (8, 128), 1) == 0, starts, 0.0)
        starts = jnp.max(jnp.max(starts, axis=1, keepdims=True), axis=0, keepdims=True)
        alarm = jnp.where(starts > 2.5, 1.0, 0.0)
    else:
        alarm = jnp.zeros((1, 1), F32)

    def terms_of(kind, start, size):
        weights = coef if kind == 0 else turned

        @pl.loop(0, width // TILE)
        def _(q):
            lanes = pl.ds(pl.multiple_of(q * TILE, TILE), TILE)
            others = held[1 - kind, :, :, lanes].reshape(RING * block_rows, TILE)
            rows = pl.ds(start * block_rows, size * block_rows)
            part[kind, rows, lanes] = dot(weights[rows], others, 1, 0)

    def at(n, k):
        return pl.ds(n * block_rows + k * slots, slots)

    def loss_of(n, k):
        return jnp.sum(losses[at(n, k)], axis=1, keepdims=True)

    def store(kind, n, k, values, loss, alarm):
        steps, extra = encode(values, loss, alarm)
        steps = steps.reshape(groups, 8, width).astype(jnp.int32)
        away[kind, n, chunk(k), :, :width] = steps.astype(jnp.int16)
        extra = extra.reshape(groups, 8, EXTRA).astype(jnp.int32)
        away[kind, n, chunk(k), :, width:] = extra.astype(jnp.int16)

    def load(ref, kind):
        value = ref[...].astype(F32).reshape(slots, width + EXTRA)
        return decode(value, width, kind == 0)

    def first(kind, k):
        return copy(
            away.at[kind, FAR, chunk(k)],
            far.at[kind, chunk(k)],
            s1.at[kind, k],
            r1.at[kind, k],
            neighbour(kind, k % 2),
        )

    def second(kind, side, k):
        return copy(
            away.at[kind, NEXT if side == 0 else PREV, chunk(k)],
            near.at[kind, side, chunk(k)],
            s2.at[kind, side, k],
            r2.at[kind, side, k],
            neighbour(kind, side),
        )

    def returned(kind, k):
        return copy(
            away.at[kind, OWN, chunk(k)],
            back.at[kind, chunk(k)],
            sb.at[kind, k],
            rb.at[kind, k],
            peer(k),
        )

    order = tuple(range(PEERS - 1, -1, -1))
    for kind in range(2):
        terms_of(kind, FAR, 1)
        for k in order:
            values = part[kind, at(FAR, k)]
            store(kind, FAR, k, values, loss_of(FAR, k) if kind == 0 else None, alarm)
            first(kind, k).start()

    for kind in range(2):
        terms_of(kind, NEXT, 2)
        for k in order:
            n = PREV if k % 2 == 0 else NEXT
            values = part[kind, at(n, k)]
            store(kind, n, k, values, loss_of(n, k) if kind == 0 else None, alarm)
            second(kind, 1 - k % 2, k).start()

    for kind in range(2):
        terms_of(kind, OWN, 1)

    for k in order:
        n = NEXT if k % 2 == 0 else PREV
        for kind in range(2):
            first(kind, k).wait_recv()
        for kind in range(2):
            values, loss, alarms = load(far.at[kind, chunk(k)], kind)
            values += part[kind, at(n, k)]
            if kind == 0:
                loss += loss_of(n, k)
                alarms = jnp.maximum(alarms, alarm)
            store(kind, n, k, values, loss, alarms)
        for kind in range(2):
            second(kind, k % 2, k).start()

    for k in order:
        for kind in range(2):
            for side in range(2):
                second(kind, side, k).wait_recv()
        for kind in range(2):
            values = part[kind, at(OWN, k)]
            loss, alarms = None, None
            if kind == 0:
                loss, alarms = loss_of(OWN, k), alarm
            for side in range(2):
                more, more_loss, more_alarms = load(near.at[kind, side, chunk(k)], kind)
                values += more
                if kind == 0:
                    loss += more_loss
                    alarms = jnp.maximum(alarms, more_alarms)
            store(kind, OWN, k, values, loss, alarms)
        for kind in range(2):
            if k == 0:
                back[kind, :groups] = away[kind, OWN, :groups]
            else:
                copy(
                    away.at[kind, OWN, chunk(k)],
                    back.at[kind, chunk(facing(k))],
                    sb.at[kind, k],
                    rb.at[kind, facing(k)],
                    peer(k),
                ).start()

    for kind, out in ((0, out_img), (1, out_txt)):
        for k in range(1, PEERS):
            returned(kind, k).wait_recv()
        steps = back[kind].astype(jnp.int32).reshape(block_rows, width + EXTRA)
        high = lax.shift_right_arithmetic(steps, 8)
        low = steps - lax.shift_left(high, 8)
        pick = layout[:, :block_rows]
        high = dot(pick, high.astype(F32).astype(BF16), 1, 0)
        low = dot(pick, low.astype(F32).astype(BF16), 1, 0)
        grad, loss, _ = decode(high * 256.0 + low, width, kind == 0)
        if kind == 0:
            loss = jnp.broadcast_to(loss * (1.0 / (RING * RING * pairs)), (pairs, pairs))
            out_loss[...] = jnp.transpose(loss)[0:1]
            alarms = jnp.max(steps[:, width:].astype(F32), axis=0, keepdims=True)
            out_alarm[...] = jnp.broadcast_to(alarms, (8, EXTRA))
        along = jnp.sum(unit[kind] * grad, axis=1, keepdims=True)
        out[...] = ((grad - unit[kind] * along) * factor[kind][:, 0:1]).astype(BF16)

    for k in range(PEERS):
        for kind in range(2):
            if k > 0:
                arrived(kind, k).wait_send()
                returned(kind, k).wait_send()
            passed(kind, k).wait_send()
            first(kind, k).wait_send()
            for side in range(2):
                gathered(kind, side, k).wait_send()
                second(kind, side, k).wait_send()


def routed(slots, scale, bias, img_feats, txt_feats, img_head, txt_head, ids, placement):
    pairs, width = img_feats.shape[0], img_head.shape[1]
    deep = img_feats.shape[1]
    wide = width + EXTRA
    block = PEERS * slots // 8
    rows = RING * PEERS * slots
    dma, vmem = pltpu.SemaphoreType.DMA, pl.BlockSpec(memory_space=pltpu.VMEM)
    smem, away = pl.BlockSpec(memory_space=pltpu.SMEM), pl.BlockSpec(memory_space=pl.ANY)
    one, two = dma((2, PEERS)), dma((2, 2, PEERS))
    return pl.pallas_call(
        functools.partial(kernel, slots),
        out_shape=(
            jax.ShapeDtypeStruct((pairs, width), BF16),
            jax.ShapeDtypeStruct((pairs, width), BF16),
            jax.ShapeDtypeStruct((1, pairs), F32),
            jax.ShapeDtypeStruct((8, EXTRA), F32),
        ),
        in_specs=[smem, smem] + [away] * 4 + [vmem] * 2,
        out_specs=(vmem,) * 4,
        scratch_shapes=[
            pltpu.VMEM((2, pairs, deep), BF16),
            pltpu.VMEM((2, deep, width), BF16),
            pltpu.VMEM((pairs, TILE), BF16),
            pltpu.VMEM((2, pairs, width), F32),
            pltpu.VMEM((2, pairs, 128), F32),
            pltpu.VMEM((2, block, 8, width), BF16),
            pltpu.VMEM((2, RING * block, 8, width), BF16),
            pltpu.VMEM((rows, rows), BF16),
            pltpu.VMEM((rows, rows), BF16),
            pltpu.VMEM((rows, 128), F32),
            pltpu.VMEM((2, rows, width), F32),
            pltpu.VMEM((2, RING, block, 8, wide), jnp.int16),
            pltpu.VMEM((2, 2, block, 8, wide), jnp.int16),
            pltpu.VMEM((2, block, 8, wide), jnp.int16),
            pltpu.VMEM((2, block, 8, wide), jnp.int16),
            dma((4,)),
        ]
        + [one] * 2
        + [two] * 2
        + [one] * 4
        + [two] * 2
        + [one] * 2,
        compiler_params=pltpu.CompilerParams(
            collective_id=slots // 8, has_side_effects=True, vmem_limit_bytes=56 * 1024 * 1024
        ),
    )(scale, bias, img_feats, txt_feats, img_head, txt_head, ids, placement)


def final_kernel(img_local, txt_local, img_head, txt_head, loss, out_img, out_txt, out_loss):
    out_img[...] = dot(img_local[...], img_head[...], 1, 1)
    out_txt[...] = dot(txt_local[...], txt_head[...], 1, 1)
    out_loss[...] = loss[...]


def final(img_local, txt_local, img_head, txt_head, loss):
    pairs, width = img_local.shape
    deep = img_head.shape[0]
    parts = 4
    step = deep // parts
    whole = pl.BlockSpec((pairs, width), lambda n: (0, 0))
    some = pl.BlockSpec((step, width), lambda n: (n, 0))
    out = pl.BlockSpec((pairs, step), lambda n: (0, n))
    line = pl.BlockSpec((1, pairs), lambda n: (0, 0))
    return pl.pallas_call(
        final_kernel,
        grid=(parts,),
        out_shape=(
            jax.ShapeDtypeStruct((pairs, deep), F32),
            jax.ShapeDtypeStruct((pairs, deep), F32),
            jax.ShapeDtypeStruct((1, pairs), F32),
        ),
        in_specs=[whole, whole, some, some, line],
        out_specs=(out, out, line),
    )(img_local, txt_local, img_head, txt_head, loss)


FAST = 24


def body(img_feats, txt_feats, img_head, txt_head, cluster_ids, placement, log_scale, bias):
    arguments = (log_scale, bias, img_feats, txt_feats, img_head, txt_head)
    arguments += (cluster_ids.reshape(1, -1), placement.reshape(1, -1))
    img_local, txt_local, loss, alarm = routed(FAST, *arguments)

    def ample():
        img_local, txt_local, loss, _ = routed(MOST, *arguments)
        return final(img_local, txt_local, img_head, txt_head, loss)

    def kept():
        return final(img_local, txt_local, img_head, txt_head, loss)

    img, txt, loss = lax.cond(alarm[0, 4] > 0.5, ample, kept)
    return img, txt, loss.reshape(-1)


def solution(mesh):
    placed = (
        P(("grp", "blk"), None),
        P(("grp", "blk"), None),
        P(),
        P(),
        P(("grp", "blk"), None),
        P(),
        P(),
        P(),
    )
    return jax.shard_map(
        body,
        mesh=mesh,
        in_specs=placed,
        out_specs=(P(("grp", "blk"), None), P(("grp", "blk"), None), P(("grp", "blk"))),
        check_vma=False,
    )
```

```python
import functools

import jax
import jax.numpy as jnp
from jax import lax
from jax.experimental import pallas as pl
from jax.experimental.pallas import tpu as pltpu
from jax.sharding import PartitionSpec as P

EPS = 1e-06
CORES = 2
RING = 4
PEERS = 8
MOST = 32
TILE = 256
EXTRA = 128
LEVELS = 32000.0
AROUND = (0, 1, 3, 2)
FACING = (0, 2, 1, 3)
OWN, NEXT, PREV, FAR = range(4)
MESH = pl.DeviceIdType.MESH
F32 = jnp.float32
BF16 = jnp.bfloat16
LOG2E = 1.4426950408889634


def dot(a, b, da, db):
    return lax.dot_general(a, b, (((da,), (db,)), ((), ())), preferred_element_type=F32)


def encode(values, loss, alarm):
    rows = values.shape[0]
    top = jnp.max(jnp.abs(values), axis=1, keepdims=True)
    grade = jnp.ceil(8.0 * jnp.log2(jnp.maximum(top, 1e-30)))
    steps = jnp.round(values * (LEVELS * jnp.exp2(-0.125 * grade)))
    lane = lax.broadcasted_iota(jnp.int32, (rows, EXTRA), 1)
    extra = jnp.where(lane == 0, grade, 0.0)
    if loss is not None:
        loss_grade = jnp.ceil(8.0 * jnp.log2(jnp.maximum(loss, 1e-30)))
        scaled = loss * (LEVELS * jnp.exp2(-0.125 * loss_grade))
        high = jnp.round(scaled)
        low = jnp.round((scaled - high) * LEVELS)
        extra = jnp.where(lane == 1, loss_grade, extra)
        extra = jnp.where(lane == 2, high, extra)
        extra = jnp.where(lane == 3, low, extra)
        extra = jnp.where(lane == 4, alarm, extra)
    return steps, extra


def decode(coded, width, with_loss):
    extra = coded[:, width:]
    values = coded[:, :width] * (jnp.exp2(0.125 * extra[:, 0:1]) * (1.0 / LEVELS))
    if not with_loss:
        return values, None, None
    scale = jnp.exp2(0.125 * extra[:, 1:2]) * (1.0 / LEVELS)
    loss = (extra[:, 2:3] + extra[:, 3:4] * (1.0 / LEVELS)) * scale
    return values, loss, extra[:, 4:5]


def kernel(
    slots,
    scale_in,
    bias_in,
    img_feats,
    txt_feats,
    img_head,
    txt_head,
    ids_in,
    placement_in,
    out_img,
    out_txt,
    out_loss,
    out_alarm,
    scale,
    bias,
    ids,
    placement,
    feats,
    head,
    layout,
    unit,
    factor,
    pack,
    held,
    coef,
    turned,
    losses,
    part,
    away,
    near,
    far,
    back,
    si,
    sa,
    ra,
    sg,
    rg,
    rh,
    sl,
    rl,
    s1,
    r1,
    s2,
    r2,
    sb,
    rb,
):
    width = img_head.shape[1]
    pairs = img_feats.shape[0]
    groups = slots // 8
    block = PEERS * groups
    block_rows = PEERS * slots
    early = 3 * block_rows // TILE
    g = lax.axis_index("grp")
    b = lax.axis_index("blk")
    x, core = lax.div(g, CORES), lax.rem(g, CORES)
    y, z = lax.div(b, RING), lax.rem(b, RING)

    def peer(k):
        to_x = lax.rem(x + AROUND[k // CORES], RING)
        return (to_x * CORES + lax.rem(core + k % CORES, CORES), b)

    def facing(k):
        return FACING[k // CORES] * CORES + k % CORES

    def neighbour(kind, side):
        step = 1 if side == 0 else RING - 1
        if kind == 0:
            return (g, y * RING + lax.rem(z + step, RING))
        return (g, lax.rem(y + step, RING) * RING + z)

    def copy(src, dst, send, recv, device):
        return pltpu.make_async_remote_copy(
            src_ref=src,
            dst_ref=dst,
            send_sem=send,
            recv_sem=recv,
            device_id=device,
            device_id_type=MESH,
        )

    def done(ref, sem):
        pltpu.make_async_copy(ref, ref, sem).wait()

    def chunk(k, at=0):
        return pl.ds(at * block + k * groups, groups)

    loads = []
    for n, (src, dst) in enumerate(
        (
            (ids_in, ids),
            (placement_in, placement),
            (img_feats, feats.at[0]),
            (img_head, head.at[0]),
            (txt_feats, feats.at[1]),
            (txt_head, head.at[1]),
            (scale_in, scale),
            (bias_in, bias),
        )
    ):
        loads.append(pltpu.make_async_copy(src, dst, si.at[n]))
        loads[-1].start()

    barrier = pltpu.get_barrier_semaphore()
    for k in range(1, PEERS):
        pl.semaphore_signal(barrier, inc=1, device_id=peer(k), device_id_type=MESH)
    for kind in range(2):
        for side in range(2):
            pl.semaphore_signal(
                barrier, inc=1, device_id=neighbour(kind, side), device_id_type=MESH
            )

    loads[0].wait()
    loads[1].wait()
    lane = lax.broadcasted_iota(jnp.int32, (pairs, 128), 1)
    row = lax.broadcasted_iota(jnp.int32, (pairs, 128), 0)
    lane_f = lane.astype(F32)
    place = placement[...].astype(F32)
    named = jnp.transpose(jnp.broadcast_to(ids[...].astype(F32), (pairs, pairs)))
    target = jnp.sum(jnp.where(named == lane_f, place, 0.0), axis=1, keepdims=True)
    team = jnp.floor(target * (1.0 / (RING * RING)))
    team_x = jnp.floor(team * (1.0 / CORES))
    dx = team_x - x.astype(F32)
    dx = jnp.where(dx < 0, dx + RING, dx)
    dx = jnp.where(dx == 2, 3.0, jnp.where(dx == 3, 2.0, dx))
    dc = team - CORES * team_x - core.astype(F32)
    where_to = CORES * dx + jnp.where(dc < 0, dc + CORES, dc)
    chosen = jnp.where(where_to == lane_f, 1.0, 0.0)
    before = jnp.where(row > lane, 1.0, 0.0).astype(BF16)
    earlier = dot(before, chosen.astype(BF16), 1, 0)
    rank = jnp.sum(earlier * chosen, axis=1, keepdims=True)
    slot = jnp.where(rank < slots, where_to * slots + rank, -1.0)
    spots = lax.broadcasted_iota(jnp.int32, (pairs, TILE), 1).astype(F32)
    layout[...] = jnp.where(spots == slot, 1.0, 0.0).astype(BF16)

    crowded = jnp.where(jnp.max(rank, axis=0, keepdims=True) >= slots, 4.0, 0.0)
    filled = dot(layout[...], jnp.ones((pairs, 128), BF16), 0, 0)[:block_rows]
    lane_block = lax.broadcasted_iota(jnp.int32, (block_rows, 128), 1)
    row_block = lax.broadcasted_iota(jnp.int32, (block_rows, 128), 0)
    mark = 2.0 - 2.0 * filled
    if slots < MOST:
        mark += jnp.where(lax.rem(row_block, slots) == 0, crowded, 0.0)
    mark = jnp.where(lane_block == 0, mark, 0.0)

    def arrived(kind, k):
        return copy(
            pack.at[kind, chunk(k)],
            held.at[kind, chunk(k)],
            sa.at[kind],
            ra.at[kind, k],
            peer(k),
        )

    def gathered(kind, side, k):
        return copy(
            held.at[kind, chunk(k)],
            held.at[kind, chunk(k, PREV if side == 0 else NEXT)],
            sg.at[kind, side],
            rg.at[kind, k] if k % 2 == side else rh.at[kind, side],
            neighbour(kind, side),
        )

    def passed(kind, k):
        side = k % 2
        return copy(
            held.at[kind, chunk(k, PREV if side == 0 else NEXT)],
            held.at[kind, chunk(k, FAR)],
            sl.at[kind],
            rl.at[kind],
            neighbour(kind, side),
        )

    def send(kind, k):
        copy(
            pack.at[kind, chunk(k)],
            held.at[kind, chunk(facing(k))],
            sa.at[kind],
            ra.at[kind, facing(k)],
            peer(k),
        ).start()

    for kind in range(2):
        loads[2 * kind + 2].wait()
        loads[2 * kind + 3].wait()
        raw = dot(feats[kind], head[kind], 1, 0)
        scale_back = lax.rsqrt(jnp.sum(raw * raw, axis=1, keepdims=True) + EPS)
        unit[kind] = raw * scale_back
        factor[kind] = jnp.broadcast_to(scale_back, (pairs, 128))
        rows = dot(layout[...], unit[kind].astype(BF16), 0, 0)[:block_rows]
        first = (rows[:, :128] + mark).reshape(block, 8, 128)
        pack[kind, :, :, :128] = first.astype(BF16)
        pack[kind, :, :, 128:] = rows[:, 128:].reshape(block, 8, width - 128).astype(BF16)
        held[kind, :groups] = pack[kind, :groups]
        if kind == 0:
            pl.semaphore_wait(barrier, PEERS - 1 + 4)
        for k in (1, 2, 4, 3, 5):
            send(kind, k)
        for side in range(2):
            gathered(kind, side, 0).start()
    for kind in range(2):
        for k in (6, 7):
            send(kind, k)

    def take(kind, k):
        arrived(kind, k).wait_recv()
        for side in range(2):
            gathered(kind, side, k).start()

    def pass_on(kind, k):
        gathered(kind, k % 2, k).wait_recv()
        passed(kind, k).start()

    take(0, 1)
    take(1, 1)
    take(0, 2)
    take(0, 4)
    pass_on(0, 0)
    take(0, 3)
    take(0, 5)
    pass_on(1, 0)
    pass_on(0, 1)
    take(1, 2)
    take(1, 4)
    pass_on(1, 1)
    pass_on(0, 2)
    take(1, 3)
    take(1, 5)
    pass_on(0, 4)
    pass_on(0, 3)
    pass_on(0, 5)
    take(0, 6)
    take(0, 7)
    pass_on(1, 2)
    pass_on(1, 4)
    take(1, 6)
    take(1, 7)
    pass_on(1, 3)
    pass_on(1, 5)
    for k in (6, 7):
        for kind in range(2):
            pass_on(kind, k)
    for kind in range(2):
        for side in range(2):
            done(held.at[kind, pl.ds(0, block // 2)], rh.at[kind, side])

    loads[6].wait()
    loads[7].wait()
    scale_t = jnp.exp(scale[...])
    shift = bias[...]
    first_lane = jnp.where(lax.broadcasted_iota(jnp.int32, (8, 128), 1) == 0, 1.0, 0.0)
    losses[...] = jnp.zeros_like(losses)

    def tile_of(i, j, with_own):
        span = TILE // 8
        images = held[0, pl.ds(i * span, span)].reshape(TILE, width)
        texts = held[1, pl.ds(j * span, span)].reshape(TILE, width)
        sims = dot(images, texts, 1, 1)
        text_first = dot(first_lane.astype(BF16), texts[:, :128], 1, 1)[0:1]
        base = jnp.where(text_first < 1.5, shift * LOG2E, -1e5)
        powers = sims * (scale_t * LOG2E) + base
        if with_own:
            row = lax.broadcasted_iota(jnp.int32, (TILE, TILE), 0)
            same = row == lax.broadcasted_iota(jnp.int32, (TILE, TILE), 1)
            same = jnp.logical_and(same, row < block_rows)
            same = jnp.logical_and(same, powers > -5e4)
            powers = jnp.where(same, -powers, powers)
        odds = jnp.exp2(powers)
        whole = 1.0 + odds
        inverse = 1.0 / whole
        terms = jnp.log(whole) + (odds - (whole - 1.0)) * inverse
        rows = pl.ds(pl.multiple_of(i * TILE, TILE), TILE)
        columns = pl.ds(pl.multiple_of(j * TILE, TILE), TILE)
        losses[rows] += terms[:, :128] + terms[:, 128:]
        weights = odds * inverse * jnp.where(images[:, 0:1].astype(F32) < 1.5, scale_t, 0.0)
        if with_own:
            weights = jnp.where(same, -weights, weights)
        coef[rows, columns] = weights.astype(BF16)
        turned[columns, rows] = jnp.transpose(weights).astype(BF16)

    tile_of(0, 0, True)

    @pl.loop(1, early * early)
    def _(t):
        tile_of(lax.div(t, early), lax.rem(t, early), False)

    for kind in range(2):
        done(held.at[kind, pl.ds(0, block)], rl.at[kind])

    @pl.loop(0, early)
    def _(t):
        tile_of(t, early, False)

    @pl.loop(0, early + 1)
    def _(t):
        tile_of(early, t, False)

    alarm = None
    if slots < MOST:
        starts = jnp.zeros((8, 128), F32)
        for kind in range(2):
            starts = jnp.maximum(starts, jnp.max(held[kind, :, :, :128].astype(F32), axis=0))
        starts = jnp.where(lax.broadcasted_iota(jnp.int32, (8, 128), 1) == 0, starts, 0.0)
        starts = jnp.max(jnp.max(starts, axis=1, keepdims=True), axis=0, keepdims=True)
        alarm = jnp.where(starts > 2.5, 1.0, 0.0)
    else:
        alarm = jnp.zeros((1, 1), F32)

    def terms_of(kind, start, size):
        weights = coef if kind == 0 else turned

        @pl.loop(0, width // TILE)
        def _(q):
            lanes = pl.ds(pl.multiple_of(q * TILE, TILE), TILE)
            others = held[1 - kind, :, :, lanes].reshape(RING * block_rows, TILE)
            rows = pl.ds(start * block_rows, size * block_rows)
            part[kind, rows, lanes] = dot(weights[rows], others, 1, 0)

    def at(n, k):
        return pl.ds(n * block_rows + k * slots, slots)

    def loss_of(n, k):
        return jnp.sum(losses[at(n, k)], axis=1, keepdims=True)

    def store(kind, n, k, values, loss, alarm):
        steps, extra = encode(values, loss, alarm)
        steps = steps.reshape(groups, 8, width).astype(jnp.int32)
        away[kind, n, chunk(k), :, :width] = steps.astype(jnp.int16)
        extra = extra.reshape(groups, 8, EXTRA).astype(jnp.int32)
        away[kind, n, chunk(k), :, width:] = extra.astype(jnp.int16)

    def load(ref, kind):
        value = ref[...].astype(F32).reshape(slots, width + EXTRA)
        return decode(value, width, kind == 0)

    def first(kind, k):
        return copy(
            away.at[kind, FAR, chunk(k)],
            far.at[k, kind],
            s1.at[kind],
            r1.at[k],
            neighbour(kind, k % 2),
        )

    def second(kind, side, k):
        return copy(
            away.at[kind, NEXT if side == 0 else PREV, chunk(k)],
            near.at[k, kind, side],
            s2.at[kind, side],
            r2.at[k],
            neighbour(kind, side),
        )

    def returned(kind, k):
        return copy(
            away.at[kind, OWN, chunk(k)],
            back.at[kind, chunk(k)],
            sb.at[kind],
            rb.at[kind],
            peer(k),
        )

    order = tuple(range(PEERS - 1, -1, -1))
    for kind in range(2):
        terms_of(kind, FAR, 1)
        for k in order:
            values = part[kind, at(FAR, k)]
            store(kind, FAR, k, values, loss_of(FAR, k) if kind == 0 else None, alarm)
            first(kind, k).start()

    for kind in range(2):
        terms_of(kind, NEXT, 2)

    def send_on(k):
        plain, mixed = (PREV, NEXT) if k % 2 == 0 else (NEXT, PREV)
        for kind in range(2):
            values = part[kind, at(plain, k)]
            store(kind, plain, k, values, loss_of(plain, k) if kind == 0 else None, alarm)
        for kind in range(2):
            second(kind, 1 - k % 2, k).start()
        done(far.at[k], r1.at[k])
        for kind in range(2):
            values, loss, alarms = load(far.at[k, kind], kind)
            values += part[kind, at(mixed, k)]
            if kind == 0:
                loss += loss_of(mixed, k)
                alarms = jnp.maximum(alarms, alarm)
            store(kind, mixed, k, values, loss, alarms)
        for kind in range(2):
            second(kind, k % 2, k).start()

    def send_back(k):
        done(near.at[k], r2.at[k])
        for kind in range(2):
            values = part[kind, at(OWN, k)]
            loss, alarms = None, None
            if kind == 0:
                loss, alarms = loss_of(OWN, k), alarm
            for side in range(2):
                more, more_loss, more_alarms = load(near.at[k, kind, side], kind)
                values += more
                if kind == 0:
                    loss += more_loss
                    alarms = jnp.maximum(alarms, more_alarms)
            store(kind, OWN, k, values, loss, alarms)
        for kind in range(2):
            if k == 0:
                back[kind, :groups] = away[kind, OWN, :groups]
            else:
                copy(
                    away.at[kind, OWN, chunk(k)],
                    back.at[kind, chunk(facing(k))],
                    sb.at[kind],
                    rb.at[kind],
                    peer(k),
                ).start()

    lag = 2
    for n, k in enumerate(order):
        send_on(k)
        if n == lag - 1:
            for kind in range(2):
                terms_of(kind, OWN, 1)
        if n >= lag:
            send_back(order[n - lag])
    for k in order[PEERS - lag :]:
        send_back(k)

    for kind, out in ((0, out_img), (1, out_txt)):
        done(back.at[kind, pl.ds(groups, block - groups)], rb.at[kind])
        steps = back[kind].astype(jnp.int32).reshape(block_rows, width + EXTRA)
        high = lax.shift_right_arithmetic(steps, 8)
        low = steps - lax.shift_left(high, 8)
        pick = layout[:, :block_rows]
        high = dot(pick, high.astype(F32).astype(BF16), 1, 0)
        low = dot(pick, low.astype(F32).astype(BF16), 1, 0)
        grad, loss, _ = decode(high * 256.0 + low, width, kind == 0)
        if kind == 0:
            loss = jnp.broadcast_to(loss * (1.0 / (RING * RING * pairs)), (pairs, pairs))
            out_loss[...] = jnp.transpose(loss)[0:1]
            out_alarm[0] = jnp.max(steps[:, width + 4 : width + 5])
        along = jnp.sum(unit[kind] * grad, axis=1, keepdims=True)
        out[...] = ((grad - unit[kind] * along) * factor[kind][:, 0:1]).astype(BF16)

    for kind in range(2):
        done(pack.at[kind, pl.ds(groups, block - groups)], sa.at[kind])
        done(held.at[kind, pl.ds(0, block)], sl.at[kind])
        done(away.at[kind, FAR], s1.at[kind])
        done(away.at[kind, OWN, pl.ds(groups, block - groups)], sb.at[kind])
        for side in range(2):
            done(held.at[kind, pl.ds(0, block)], sg.at[kind, side])
            done(away.at[kind, FAR], s2.at[kind, side])


def routed(slots, scale, bias, img_feats, txt_feats, img_head, txt_head, ids, placement):
    pairs, width = img_feats.shape[0], img_head.shape[1]
    deep = img_feats.shape[1]
    wide = width + EXTRA
    block = PEERS * slots // 8
    rows = RING * PEERS * slots
    dma, vmem = pltpu.SemaphoreType.DMA, pl.BlockSpec(memory_space=pltpu.VMEM)
    smem, away = pl.BlockSpec(memory_space=pltpu.SMEM), pl.BlockSpec(memory_space=pl.ANY)
    return pl.pallas_call(
        functools.partial(kernel, slots),
        out_shape=(
            jax.ShapeDtypeStruct((pairs, width), BF16),
            jax.ShapeDtypeStruct((pairs, width), BF16),
            jax.ShapeDtypeStruct((1, pairs), F32),
            jax.ShapeDtypeStruct((1,), jnp.int32),
        ),
        in_specs=[away] * 8,
        out_specs=(vmem, vmem, vmem, smem),
        scratch_shapes=[
            pltpu.VMEM((1, 1), F32),
            pltpu.VMEM((1, 1), F32),
            pltpu.VMEM((1, pairs), jnp.int32),
            pltpu.VMEM((1, pairs), jnp.int32),
            pltpu.VMEM((2, pairs, deep), BF16),
            pltpu.VMEM((2, deep, width), BF16),
            pltpu.VMEM((pairs, TILE), BF16),
            pltpu.VMEM((2, pairs, width), F32),
            pltpu.VMEM((2, pairs, 128), F32),
            pltpu.VMEM((2, block, 8, width), BF16),
            pltpu.VMEM((2, RING * block, 8, width), BF16),
            pltpu.VMEM((rows, rows), BF16),
            pltpu.VMEM((rows, rows), BF16),
            pltpu.VMEM((rows, 128), F32),
            pltpu.VMEM((2, rows, width), F32),
            pltpu.VMEM((2, RING, block, 8, wide), jnp.int16),
            pltpu.VMEM((PEERS, 2, 2, slots // 8, 8, wide), jnp.int16),
            pltpu.VMEM((PEERS, 2, slots // 8, 8, wide), jnp.int16),
            pltpu.VMEM((2, block, 8, wide), jnp.int16),
            dma((8,)),
            dma((2,)),
            dma((2, PEERS)),
            dma((2, 2)),
            dma((2, PEERS)),
            dma((2, 2)),
            dma((2,)),
            dma((2,)),
            dma((2,)),
            dma((PEERS,)),
            dma((2, 2)),
            dma((PEERS,)),
            dma((2,)),
            dma((2,)),
        ],
        compiler_params=pltpu.CompilerParams(
            collective_id=slots // 8,
            has_side_effects=True,
            vmem_limit_bytes=(48 if slots == MOST else 40) * 1024 * 1024,
        ),
    )(scale, bias, img_feats, txt_feats, img_head, txt_head, ids, placement)


def final_kernel(
    img_local, txt_local, img_head, txt_head, loss, out_img, out_txt, out_loss, done, sems
):
    copies = []
    for kind, (local, head, out) in enumerate(
        ((img_local, img_head, out_img), (txt_local, txt_head, out_txt))
    ):
        done[kind] = dot(local[...], head[...], 1, 1)
        copies.append(pltpu.make_async_copy(done.at[kind], out, sems.at[kind]))
        copies[-1].start()
    out_loss[...] = loss[...]
    for copy in copies:
        copy.wait()


def final(img_local, txt_local, img_head, txt_head, loss):
    pairs, width = img_local.shape
    deep = img_head.shape[0]
    vmem, away = pl.BlockSpec(memory_space=pltpu.VMEM), pl.BlockSpec(memory_space=pl.ANY)
    return pl.pallas_call(
        final_kernel,
        out_shape=(
            jax.ShapeDtypeStruct((pairs, deep), F32),
            jax.ShapeDtypeStruct((pairs, deep), F32),
            jax.ShapeDtypeStruct((1, pairs), F32),
        ),
        in_specs=[vmem] * 5,
        out_specs=(away, away, vmem),
        scratch_shapes=[pltpu.VMEM((2, pairs, deep), F32), pltpu.SemaphoreType.DMA((2,))],
        compiler_params=pltpu.CompilerParams(vmem_limit_bytes=12 * 1024 * 1024),
    )(img_local, txt_local, img_head, txt_head, loss)


FAST = 24


def body(img_feats, txt_feats, img_head, txt_head, cluster_ids, placement, log_scale, bias):
    arguments = (log_scale.reshape(1, 1), bias.reshape(1, 1), img_feats, txt_feats, img_head, txt_head)
    arguments += (cluster_ids.reshape(1, -1), placement.reshape(1, -1))
    img_local, txt_local, loss, alarm = routed(FAST, *arguments)

    def ample():
        img_local, txt_local, loss, _ = routed(MOST, *arguments)
        return final(img_local, txt_local, img_head, txt_head, loss)

    def kept():
        return final(img_local, txt_local, img_head, txt_head, loss)

    img, txt, loss = lax.cond(alarm[0] > 0, ample, kept)
    return img, txt, loss.reshape(-1)


def solution(mesh):
    placed = (
        P(("grp", "blk"), None),
        P(("grp", "blk"), None),
        P(),
        P(),
        P(("grp", "blk"), None),
        P(),
        P(),
        P(),
    )
    return jax.shard_map(
        body,
        mesh=mesh,
        in_specs=placed,
        out_specs=(P(("grp", "blk"), None), P(("grp", "blk"), None), P(("grp", "blk"))),
        check_vma=False,
    )
```

```python
import functools

import jax
import jax.numpy as jnp
from jax import lax
from jax.experimental import pallas as pl
from jax.experimental.pallas import tpu as pltpu
from jax.sharding import PartitionSpec as P

EPS = 1e-06
CORES = 2
RING = 4
PEERS = 8
MOST = 32
TILE = 256
EXTRA = 128
LEVELS = 32000.0
AROUND = (0, 1, 3, 2)
ARRIVALS = (1, 2, 4, 3, 5, 6, 7)
SOON = 3
LAG = 6
FACING = (0, 2, 1, 3)
OWN, NEXT, PREV, FAR = range(4)
MESH = pl.DeviceIdType.MESH
F32 = jnp.float32
BF16 = jnp.bfloat16
LOG2E = 1.4426950408889634


def dot(a, b, da, db):
    return lax.dot_general(a, b, (((da,), (db,)), ((), ())), preferred_element_type=F32)


def encode(values, top, loss, alarm):
    rows = values.shape[0]
    grade = jnp.ceil(8.0 * jnp.log2(jnp.maximum(top, 1e-30)))
    steps = jnp.round(values * (LEVELS * jnp.exp2(-0.125 * grade)))
    lane = lax.broadcasted_iota(jnp.int32, (rows, EXTRA), 1)
    extra = jnp.where(lane == 0, grade, 0.0)
    if loss is not None:
        loss_grade = jnp.ceil(8.0 * jnp.log2(jnp.maximum(loss, 1e-30)))
        scaled = loss * (LEVELS * jnp.exp2(-0.125 * loss_grade))
        high = jnp.round(scaled)
        low = jnp.round((scaled - high) * LEVELS)
        extra = jnp.where(lane == 1, loss_grade, extra)
        extra = jnp.where(lane == 2, high, extra)
        extra = jnp.where(lane == 3, low, extra)
        extra = jnp.where(lane == 4, alarm, extra)
    return steps, extra


def decode(coded, width, with_loss):
    extra = coded[:, width:]
    top = jnp.exp2(0.125 * extra[:, 0:1])
    values = coded[:, :width] * (top * (1.0 / LEVELS))
    if not with_loss:
        return values, top, None, None
    scale = jnp.exp2(0.125 * extra[:, 1:2]) * (1.0 / LEVELS)
    loss = (extra[:, 2:3] + extra[:, 3:4] * (1.0 / LEVELS)) * scale
    return values, top, loss, extra[:, 4:5]


def kernel(
    slots,
    scale_in,
    bias_in,
    img_feats,
    txt_feats,
    img_head,
    txt_head,
    ids_in,
    placement_in,
    out_img,
    out_txt,
    out_loss,
    out_alarm,
    scale,
    bias,
    ids,
    placement,
    feats,
    head,
    layout,
    unit,
    factor,
    pack,
    held,
    coef,
    turned,
    losses,
    part,
    tops,
    away,
    near,
    far,
    back,
    si,
    sa,
    ra,
    sg,
    rg,
    rh,
    sl,
    rl,
    s1,
    r1,
    s2,
    r2,
    sb,
    rb,
):
    width = img_head.shape[1]
    pairs = img_feats.shape[0]
    groups = slots // 8
    block = PEERS * groups
    block_rows = PEERS * slots
    early = 3 * block_rows // TILE
    g = lax.axis_index("grp")
    b = lax.axis_index("blk")
    x, core = lax.div(g, CORES), lax.rem(g, CORES)
    y, z = lax.div(b, RING), lax.rem(b, RING)

    def peer(k):
        to_x = lax.rem(x + AROUND[k // CORES], RING)
        return (to_x * CORES + lax.rem(core + k % CORES, CORES), b)

    def facing(k):
        return FACING[k // CORES] * CORES + k % CORES

    def neighbour(kind, side):
        step = 1 if side == 0 else RING - 1
        if kind == 0:
            return (g, y * RING + lax.rem(z + step, RING))
        return (g, lax.rem(y + step, RING) * RING + z)

    def copy(src, dst, send, recv, device):
        return pltpu.make_async_remote_copy(
            src_ref=src,
            dst_ref=dst,
            send_sem=send,
            recv_sem=recv,
            device_id=device,
            device_id_type=MESH,
        )

    def done(ref, sem):
        pltpu.make_async_copy(ref, ref, sem).wait()

    def chunk(k, at=0):
        return pl.ds(at * block + k * groups, groups)

    loads = []
    for n, (src, dst) in enumerate(
        (
            (ids_in, ids),
            (placement_in, placement),
            (img_feats, feats.at[0]),
            (img_head, head.at[0]),
            (txt_feats, feats.at[1]),
            (txt_head, head.at[1]),
            (scale_in, scale),
            (bias_in, bias),
        )
    ):
        loads.append(pltpu.make_async_copy(src, dst, si.at[n]))
        loads[-1].start()

    barrier = pltpu.get_barrier_semaphore()
    for k in range(1, PEERS):
        pl.semaphore_signal(barrier, inc=1, device_id=peer(k), device_id_type=MESH)
    for kind in range(2):
        for side in range(2):
            pl.semaphore_signal(
                barrier, inc=1, device_id=neighbour(kind, side), device_id_type=MESH
            )

    loads[0].wait()
    loads[1].wait()
    lane = lax.broadcasted_iota(jnp.int32, (pairs, 128), 1)
    row = lax.broadcasted_iota(jnp.int32, (pairs, 128), 0)
    lane_f = lane.astype(F32)
    place = placement[...].astype(F32)
    named = jnp.transpose(jnp.broadcast_to(ids[...].astype(F32), (pairs, pairs)))
    target = jnp.sum(jnp.where(named == lane_f, place, 0.0), axis=1, keepdims=True)
    team = jnp.floor(target * (1.0 / (RING * RING)))
    team_x = jnp.floor(team * (1.0 / CORES))
    dx = team_x - x.astype(F32)
    dx = jnp.where(dx < 0, dx + RING, dx)
    dx = jnp.where(dx == 2, 3.0, jnp.where(dx == 3, 2.0, dx))
    dc = team - CORES * team_x - core.astype(F32)
    where_to = CORES * dx + jnp.where(dc < 0, dc + CORES, dc)
    chosen = jnp.where(where_to == lane_f, 1.0, 0.0)
    before = jnp.where(row > lane, 1.0, 0.0).astype(BF16)
    earlier = dot(before, chosen.astype(BF16), 1, 0)
    rank = jnp.sum(earlier * chosen, axis=1, keepdims=True)
    slot = jnp.where(rank < slots, where_to * slots + rank, -1.0)
    spots = lax.broadcasted_iota(jnp.int32, (pairs, TILE), 1).astype(F32)
    layout[...] = jnp.where(spots == slot, 1.0, 0.0).astype(BF16)

    crowded = jnp.where(jnp.max(rank, axis=0, keepdims=True) >= slots, 4.0, 0.0)
    filled = dot(layout[...], jnp.ones((pairs, 128), BF16), 0, 0)[:block_rows]
    lane_block = lax.broadcasted_iota(jnp.int32, (block_rows, 128), 1)
    row_block = lax.broadcasted_iota(jnp.int32, (block_rows, 128), 0)
    mark = 2.0 - 2.0 * filled
    if slots < MOST:
        mark += jnp.where(lax.rem(row_block, slots) == 0, crowded, 0.0)
    mark = jnp.where(lane_block == 0, mark, 0.0)

    def arrived(kind, k):
        return copy(
            pack.at[kind, chunk(k)],
            held.at[kind, chunk(k)],
            sa.at[kind],
            ra.at[kind, k],
            peer(k),
        )

    def gathered(kind, side, k):
        return copy(
            held.at[kind, chunk(k)],
            held.at[kind, chunk(k, PREV if side == 0 else NEXT)],
            sg.at[kind, side],
            rg.at[kind, k] if k % 2 == side else rh.at[kind, side],
            neighbour(kind, side),
        )

    def passed(kind, k):
        side = k % 2
        return copy(
            held.at[kind, chunk(k, PREV if side == 0 else NEXT)],
            held.at[kind, chunk(k, FAR)],
            sl.at[kind],
            rl.at[kind],
            neighbour(kind, side),
        )

    def send(kind, k):
        copy(
            pack.at[kind, chunk(k)],
            held.at[kind, chunk(facing(k))],
            sa.at[kind],
            ra.at[kind, facing(k)],
            peer(k),
        ).start()

    for kind in range(2):
        loads[2 * kind + 2].wait()
        loads[2 * kind + 3].wait()
        raw = dot(feats[kind], head[kind], 1, 0)
        scale_back = lax.rsqrt(jnp.sum(raw * raw, axis=1, keepdims=True) + EPS)
        unit[kind] = raw * scale_back
        factor[kind] = jnp.broadcast_to(scale_back, (pairs, 128))
        rows = dot(layout[...], unit[kind].astype(BF16), 0, 0)[:block_rows]
        first = (rows[:, :128] + mark).reshape(block, 8, 128)
        pack[kind, :, :, :128] = first.astype(BF16)
        pack[kind, :, :, 128:] = rows[:, 128:].reshape(block, 8, width - 128).astype(BF16)
        held[kind, :groups] = pack[kind, :groups]
        if kind == 0:
            pl.semaphore_wait(barrier, PEERS - 1 + 4)
        for k in ARRIVALS[:SOON]:
            send(kind, k)
        for side in range(2):
            gathered(kind, side, 0).start()
    for k in ARRIVALS[SOON:]:
        for kind in range(2):
            send(kind, k)

    def take(kind, k):
        arrived(kind, k).wait_recv()
        for side in range(2):
            gathered(kind, side, k).start()

    def pass_on(kind, k):
        gathered(kind, k % 2, k).wait_recv()
        passed(kind, k).start()

    takes = [(kind, k) for k in ARRIVALS for kind in range(2)]
    passes = [(kind, k) for k in (0,) + ARRIVALS for kind in range(2)]
    for n, one in enumerate(takes):
        take(*one)
        if n >= LAG:
            pass_on(*passes[n - LAG])
    for one in passes[len(takes) - LAG :]:
        pass_on(*one)

    for kind in range(2):
        for side in range(2):
            done(held.at[kind, pl.ds(0, block // 2)], rh.at[kind, side])

    loads[6].wait()
    loads[7].wait()
    scale_t = jnp.exp(scale[...])
    shift = bias[...]
    first_lane = jnp.where(lax.broadcasted_iota(jnp.int32, (8, 128), 1) == 0, 1.0, 0.0)
    losses[...] = jnp.zeros_like(losses)

    def tile_of(i, j, with_own):
        span = TILE // 8
        images = held[0, pl.ds(i * span, span)].reshape(TILE, width)
        texts = held[1, pl.ds(j * span, span)].reshape(TILE, width)
        sims = dot(images, texts, 1, 1)
        text_first = dot(first_lane.astype(BF16), texts[:, :128], 1, 1)[0:1]
        base = jnp.where(text_first < 1.5, shift * LOG2E, -1e5)
        powers = sims * (scale_t * LOG2E) + base
        if with_own:
            row = lax.broadcasted_iota(jnp.int32, (TILE, TILE), 0)
            same = row == lax.broadcasted_iota(jnp.int32, (TILE, TILE), 1)
            same = jnp.logical_and(same, row < block_rows)
            same = jnp.logical_and(same, powers > -5e4)
            powers = jnp.where(same, -powers, powers)
        odds = jnp.exp2(powers)
        whole = 1.0 + odds
        inverse = 1.0 / whole
        terms = jnp.log(whole) + (odds - (whole - 1.0)) * inverse
        rows = pl.ds(i * TILE, TILE)
        columns = pl.ds(j * TILE, TILE)
        losses[rows] += terms[:, :128] + terms[:, 128:]
        weights = odds * inverse * jnp.where(images[:, 0:1].astype(F32) < 1.5, scale_t, 0.0)
        if with_own:
            weights = jnp.where(same, -weights, weights)
        coef[rows, columns] = weights.astype(BF16)
        turned[columns, rows] = jnp.transpose(weights).astype(BF16)

    tile_of(0, 0, True)

    for t in range(1, early * early):
        tile_of(t // early, t % early, False)

    for kind in range(2):
        done(held.at[kind, pl.ds(0, block)], rl.at[kind])

    for t in range(early):
        tile_of(t, early, False)
    for t in range(early + 1):
        tile_of(early, t, False)

    alarm = None
    if slots < MOST:
        starts = jnp.zeros((8, 128), F32)
        for kind in range(2):
            starts = jnp.maximum(starts, jnp.max(held[kind, :, :, :128].astype(F32), axis=0))
        starts = jnp.where(lax.broadcasted_iota(jnp.int32, (8, 128), 1) == 0, starts, 0.0)
        starts = jnp.max(jnp.max(starts, axis=1, keepdims=True), axis=0, keepdims=True)
        alarm = jnp.where(starts > 2.5, 1.0, 0.0)
    else:
        alarm = jnp.zeros((1, 1), F32)

    def terms_of(kind, start, size):
        weights = coef if kind == 0 else turned

        for q in range(width // TILE):
            lanes = pl.ds(q * TILE, TILE)
            others = held[1 - kind, :, :, lanes].reshape(RING * block_rows, TILE)
            rows = pl.ds(start * block_rows, size * block_rows)
            part[kind, rows, lanes] = dot(weights[rows], others, 1, 0)

        rows = pl.ds(start * block_rows, size * block_rows)
        top = jnp.max(jnp.abs(part[kind, rows]), axis=1, keepdims=True)
        tops[kind, rows] = jnp.broadcast_to(top, (size * block_rows, 128))

    def at(n, k):
        return pl.ds(n * block_rows + k * slots, slots)

    total = jnp.sum(losses[...], axis=1, keepdims=True)
    losses[...] = jnp.broadcast_to(total, losses.shape)

    def mine(kind, n, k):
        rows = at(n, k)
        loss = losses[rows][:, 0:1] if kind == 0 else None
        alarms = alarm if kind == 0 else None
        return part[kind, rows], tops[kind, rows][:, 0:1], loss, alarms

    def both(one, other):
        sums = [a if b is None else a + b for a, b in zip(one[:3], other[:3])]
        return (*sums, None if one[3] is None else jnp.maximum(one[3], other[3]))

    def store(kind, n, k, terms):
        steps, extra = encode(*terms)
        steps = steps.reshape(groups, 8, width).astype(jnp.int32)
        away[kind, n, chunk(k), :, :width] = steps.astype(jnp.int16)
        extra = extra.reshape(groups, 8, EXTRA).astype(jnp.int32)
        away[kind, n, chunk(k), :, width:] = extra.astype(jnp.int16)

    def load(ref, kind):
        value = ref[...].astype(F32).reshape(slots, width + EXTRA)
        return decode(value, width, kind == 0)

    def first(kind, k):
        return copy(
            away.at[kind, FAR, chunk(k)],
            far.at[k, kind],
            s1.at[kind],
            r1.at[k],
            neighbour(kind, k % 2),
        )

    def second(kind, side, k):
        return copy(
            away.at[kind, NEXT if side == 0 else PREV, chunk(k)],
            near.at[k, kind, side],
            s2.at[kind, side],
            r2.at[k],
            neighbour(kind, side),
        )

    def returned(kind, k):
        return copy(
            away.at[kind, OWN, chunk(k)],
            back.at[kind, chunk(k)],
            sb.at[kind],
            rb.at[kind],
            peer(k),
        )

    def plain(k):
        return PREV if k % 2 == 0 else NEXT

    def mixed(k):
        return NEXT if k % 2 == 0 else PREV

    couples = ((7, 6), (5, 2), (4, 3), (1, 0))
    order = tuple(k for couple in couples for k in couple)
    for kind in range(2):
        terms_of(kind, FAR, 1)
        for some in (order[:2], order[2:]):
            for k in some:
                store(kind, FAR, k, mine(kind, FAR, k))
            for k in some[:4]:
                first(kind, k).start()

    for kind in range(2):
        terms_of(kind, NEXT, 2)
        for k in order:
            store(kind, plain(k), k, mine(kind, plain(k), k))
        for k in order[:2]:
            second(kind, 1 - k % 2, k).start()

    def send_on(couple):
        for k in couple:
            done(far.at[k], r1.at[k])
        for k in couple:
            for kind in range(2):
                more = load(far.at[k, kind], kind)
                store(kind, mixed(k), k, both(mine(kind, mixed(k), k), more))
        for k in couple:
            for kind in range(2):
                second(kind, k % 2, k).start()

    def send_back(k):
        done(near.at[k], r2.at[k])
        for kind in range(2):
            terms = mine(kind, OWN, k)
            for side in range(2):
                terms = both(terms, load(near.at[k, kind, side], kind))
            store(kind, OWN, k, terms)
        for kind in range(2):
            if k == 0:
                back[kind, :groups] = away[kind, OWN, :groups]
            else:
                copy(
                    away.at[kind, OWN, chunk(k)],
                    back.at[kind, chunk(facing(k))],
                    sb.at[kind],
                    rb.at[kind],
                    peer(k),
                ).start()

    for n, couple in enumerate(couples):
        send_on(couple)
        if n == 0:
            for kind in range(2):
                for k in order[6:]:
                    first(kind, k).start()
        if n + 1 < len(couples):
            for kind in range(2):
                for k in couples[n + 1]:
                    second(kind, 1 - k % 2, k).start()
        if n == 0:
            for kind in range(2):
                terms_of(kind, OWN, 1)
        else:
            for k in couples[n - 1]:
                send_back(k)
    for k in couples[-1]:
        send_back(k)

    for kind, out in ((0, out_img), (1, out_txt)):
        done(back.at[kind, pl.ds(groups, block - groups)], rb.at[kind])
        steps = back[kind].astype(jnp.int32).reshape(block_rows, width + EXTRA)
        high = lax.shift_right_arithmetic(steps, 8)
        low = steps - lax.shift_left(high, 8)
        pick = layout[:, :block_rows]
        high = dot(pick, high.astype(F32).astype(BF16), 1, 0)
        low = dot(pick, low.astype(F32).astype(BF16), 1, 0)
        grad, _, loss, _ = decode(high * 256.0 + low, width, kind == 0)
        if kind == 0:
            loss = jnp.broadcast_to(loss * (1.0 / (RING * RING * pairs)), (pairs, pairs))
            out_loss[...] = jnp.transpose(loss)[0:1]
            out_alarm[0] = jnp.max(steps[:, width + 4 : width + 5])
        along = jnp.sum(unit[kind] * grad, axis=1, keepdims=True)
        out[...] = ((grad - unit[kind] * along) * factor[kind][:, 0:1]).astype(BF16)

    for kind in range(2):
        done(pack.at[kind, pl.ds(groups, block - groups)], sa.at[kind])
        done(held.at[kind, pl.ds(0, block)], sl.at[kind])
        done(away.at[kind, FAR], s1.at[kind])
        done(away.at[kind, OWN, pl.ds(groups, block - groups)], sb.at[kind])
        for side in range(2):
            done(held.at[kind, pl.ds(0, block)], sg.at[kind, side])
            done(away.at[kind, FAR], s2.at[kind, side])


def routed(slots, scale, bias, img_feats, txt_feats, img_head, txt_head, ids, placement):
    pairs, width = img_feats.shape[0], img_head.shape[1]
    deep = img_feats.shape[1]
    wide = width + EXTRA
    block = PEERS * slots // 8
    rows = RING * PEERS * slots
    dma, vmem = pltpu.SemaphoreType.DMA, pl.BlockSpec(memory_space=pltpu.VMEM)
    smem, away = pl.BlockSpec(memory_space=pltpu.SMEM), pl.BlockSpec(memory_space=pl.ANY)
    return pl.pallas_call(
        functools.partial(kernel, slots),
        out_shape=(
            jax.ShapeDtypeStruct((pairs, width), BF16),
            jax.ShapeDtypeStruct((pairs, width), BF16),
            jax.ShapeDtypeStruct((1, pairs), F32),
            jax.ShapeDtypeStruct((1,), jnp.int32),
        ),
        in_specs=[away] * 8,
        out_specs=(vmem, vmem, vmem, smem),
        scratch_shapes=[
            pltpu.VMEM((1, 1), F32),
            pltpu.VMEM((1, 1), F32),
            pltpu.VMEM((1, pairs), jnp.int32),
            pltpu.VMEM((1, pairs), jnp.int32),
            pltpu.VMEM((2, pairs, deep), BF16),
            pltpu.VMEM((2, deep, width), BF16),
            pltpu.VMEM((pairs, TILE), BF16),
            pltpu.VMEM((2, pairs, width), F32),
            pltpu.VMEM((2, pairs, 128), F32),
            pltpu.VMEM((2, block, 8, width), BF16),
            pltpu.VMEM((2, RING * block, 8, width), BF16),
            pltpu.VMEM((rows, rows), BF16),
            pltpu.VMEM((rows, rows), BF16),
            pltpu.VMEM((rows, 128), F32),
            pltpu.VMEM((2, rows, width), F32),
            pltpu.VMEM((2, rows, 128), F32),
            pltpu.VMEM((2, RING, block, 8, wide), jnp.int16),
            pltpu.VMEM((PEERS, 2, 2, slots // 8, 8, wide), jnp.int16),
            pltpu.VMEM((PEERS, 2, slots // 8, 8, wide), jnp.int16),
            pltpu.VMEM((2, block, 8, wide), jnp.int16),
            dma((8,)),
            dma((2,)),
            dma((2, PEERS)),
            dma((2, 2)),
            dma((2, PEERS)),
            dma((2, 2)),
            dma((2,)),
            dma((2,)),
            dma((2,)),
            dma((PEERS,)),
            dma((2, 2)),
            dma((PEERS,)),
            dma((2,)),
            dma((2,)),
        ],
        compiler_params=pltpu.CompilerParams(
            collective_id=slots // 8,
            has_side_effects=True,
            vmem_limit_bytes=(48 if slots == MOST else 40) * 1024 * 1024,
        ),
    )(scale, bias, img_feats, txt_feats, img_head, txt_head, ids, placement)


def final_kernel(
    img_local, txt_local, img_head, txt_head, loss, out_img, out_txt, out_loss, done, sems
):
    copies = []
    for kind, (local, head, out) in enumerate(
        ((img_local, img_head, out_img), (txt_local, txt_head, out_txt))
    ):
        done[kind] = dot(local[...], head[...], 1, 1)
        copies.append(pltpu.make_async_copy(done.at[kind], out, sems.at[kind]))
        copies[-1].start()
    out_loss[...] = loss[...]
    for copy in copies:
        copy.wait()


def final(img_local, txt_local, img_head, txt_head, loss):
    pairs, width = img_local.shape
    deep = img_head.shape[0]
    vmem, away = pl.BlockSpec(memory_space=pltpu.VMEM), pl.BlockSpec(memory_space=pl.ANY)
    return pl.pallas_call(
        final_kernel,
        out_shape=(
            jax.ShapeDtypeStruct((pairs, deep), F32),
            jax.ShapeDtypeStruct((pairs, deep), F32),
            jax.ShapeDtypeStruct((1, pairs), F32),
        ),
        in_specs=[vmem] * 5,
        out_specs=(away, away, vmem),
        scratch_shapes=[pltpu.VMEM((2, pairs, deep), F32), pltpu.SemaphoreType.DMA((2,))],
        compiler_params=pltpu.CompilerParams(vmem_limit_bytes=12 * 1024 * 1024),
    )(img_local, txt_local, img_head, txt_head, loss)


FAST = 24


def body(img_feats, txt_feats, img_head, txt_head, cluster_ids, placement, log_scale, bias):
    arguments = (log_scale.reshape(1, 1), bias.reshape(1, 1), img_feats, txt_feats, img_head, txt_head)
    arguments += (cluster_ids.reshape(1, -1), placement.reshape(1, -1))
    img_local, txt_local, loss, alarm = routed(FAST, *arguments)

    def ample():
        img_local, txt_local, loss, _ = routed(MOST, *arguments)
        return final(img_local, txt_local, img_head, txt_head, loss)

    def kept():
        return final(img_local, txt_local, img_head, txt_head, loss)

    img, txt, loss = lax.cond(alarm[0] > 0, ample, kept)
    return img, txt, loss.reshape(-1)


def solution(mesh):
    placed = (
        P(("grp", "blk"), None),
        P(("grp", "blk"), None),
        P(),
        P(),
        P(("grp", "blk"), None),
        P(),
        P(),
        P(),
    )
    return jax.shard_map(
        body,
        mesh=mesh,
        in_specs=placed,
        out_specs=(P(("grp", "blk"), None), P(("grp", "blk"), None), P(("grp", "blk"))),
        check_vma=False,
    )
```

```python
import functools

import jax
import jax.numpy as jnp
from jax import lax
from jax.experimental import pallas as pl
from jax.experimental.pallas import tpu as pltpu
from jax.sharding import PartitionSpec as P

EPS = 1e-06
CORES = 2
RING = 4
PEERS = 8
MOST = 32
TILE = 256
EXTRA = 128
LEVELS = 32000.0
AROUND = (0, 1, 3, 2)
ARRIVALS = (1, 2, 4, 3, 5, 6, 7)
SOON = 3
LAG = 6
FACING = (0, 2, 1, 3)
OWN, NEXT, PREV, FAR = range(4)
MESH = pl.DeviceIdType.MESH
F32 = jnp.float32
BF16 = jnp.bfloat16
LOG2E = 1.4426950408889634


def dot(a, b, da, db):
    return lax.dot_general(a, b, (((da,), (db,)), ((), ())), preferred_element_type=F32)


def encode(values, top, loss, alarm):
    grade = jnp.ceil(8.0 * jnp.log2(jnp.maximum(top, 1e-30)))
    scale = LEVELS * jnp.exp2(-0.125 * grade)
    steps = [jnp.round(values[:, n : n + EXTRA] * scale) for n in range(0, values.shape[1], EXTRA)]
    fields = [grade]
    if loss is not None:
        loss_grade = jnp.ceil(8.0 * jnp.log2(jnp.maximum(loss, 1e-30)))
        scaled = loss * (LEVELS * jnp.exp2(-0.125 * loss_grade))
        high = jnp.round(scaled)
        low = jnp.round((scaled - high) * LEVELS)
        fields += [loss_grade, high, low, alarm]
    lane = lax.broadcasted_iota(jnp.int32, (8, EXTRA), 1)
    extra = jnp.zeros((8, EXTRA), F32)
    for r in range(values.shape[0] // 8):
        for f, field in enumerate(fields):
            extra = jnp.where(lane == 8 * r + f, field[8 * r : 8 * r + 8], extra)
    return steps, extra


def loss_from(loss_grade, high, low):
    scale = jnp.exp2(0.125 * loss_grade) * (1.0 / LEVELS)
    return (high + low * (1.0 / LEVELS)) * scale


def kernel(
    slots,
    scale_in,
    bias_in,
    img_feats,
    txt_feats,
    img_head,
    txt_head,
    ids_in,
    placement_in,
    out_img,
    out_txt,
    out_loss,
    out_alarm,
    scale,
    bias,
    ids,
    placement,
    feats,
    head,
    layout,
    unit,
    factor,
    pack,
    held,
    coef,
    turned,
    losses,
    part,
    tops,
    away,
    near,
    far,
    back,
    si,
    sa,
    ra,
    sg,
    rg,
    rh,
    sl,
    rl,
    s1,
    r1,
    s2,
    r2,
    sb,
    rb,
):
    width = img_head.shape[1]
    pairs = img_feats.shape[0]
    groups = slots // 8
    block = PEERS * groups
    block_rows = PEERS * slots
    early = 3 * block_rows // TILE
    g = lax.axis_index("grp")
    b = lax.axis_index("blk")
    x, core = lax.div(g, CORES), lax.rem(g, CORES)
    y, z = lax.div(b, RING), lax.rem(b, RING)

    def peer(k):
        to_x = lax.rem(x + AROUND[k // CORES], RING)
        return (to_x * CORES + lax.rem(core + k % CORES, CORES), b)

    def facing(k):
        return FACING[k // CORES] * CORES + k % CORES

    def neighbour(kind, side):
        step = 1 if side == 0 else RING - 1
        if kind == 0:
            return (g, y * RING + lax.rem(z + step, RING))
        return (g, lax.rem(y + step, RING) * RING + z)

    def copy(src, dst, send, recv, device):
        return pltpu.make_async_remote_copy(
            src_ref=src,
            dst_ref=dst,
            send_sem=send,
            recv_sem=recv,
            device_id=device,
            device_id_type=MESH,
        )

    def done(ref, sem):
        pltpu.make_async_copy(ref, ref, sem).wait()

    def chunk(k, at=0):
        return pl.ds(at * block + k * groups, groups)

    loads = []
    for n, (src, dst) in enumerate(
        (
            (ids_in, ids),
            (placement_in, placement),
            (img_feats, feats.at[0]),
            (img_head, head.at[0]),
            (txt_feats, feats.at[1]),
            (txt_head, head.at[1]),
            (scale_in, scale),
            (bias_in, bias),
        )
    ):
        loads.append(pltpu.make_async_copy(src, dst, si.at[n]))
        loads[-1].start()

    barrier = pltpu.get_barrier_semaphore()
    for k in range(1, PEERS):
        pl.semaphore_signal(barrier, inc=1, device_id=peer(k), device_id_type=MESH)
    for kind in range(2):
        for side in range(2):
            pl.semaphore_signal(
                barrier, inc=1, device_id=neighbour(kind, side), device_id_type=MESH
            )

    loads[0].wait()
    loads[1].wait()
    lane = lax.broadcasted_iota(jnp.int32, (pairs, 128), 1)
    row = lax.broadcasted_iota(jnp.int32, (pairs, 128), 0)
    lane_f = lane.astype(F32)
    place = placement[...].astype(F32)
    named = jnp.transpose(jnp.broadcast_to(ids[...].astype(F32), (pairs, pairs)))
    target = jnp.sum(jnp.where(named == lane_f, place, 0.0), axis=1, keepdims=True)
    team = jnp.floor(target * (1.0 / (RING * RING)))
    team_x = jnp.floor(team * (1.0 / CORES))
    dx = team_x - x.astype(F32)
    dx = jnp.where(dx < 0, dx + RING, dx)
    dx = jnp.where(dx == 2, 3.0, jnp.where(dx == 3, 2.0, dx))
    dc = team - CORES * team_x - core.astype(F32)
    where_to = CORES * dx + jnp.where(dc < 0, dc + CORES, dc)
    chosen = jnp.where(where_to == lane_f, 1.0, 0.0)
    before = jnp.where(row > lane, 1.0, 0.0).astype(BF16)
    earlier = dot(before, chosen.astype(BF16), 1, 0)
    rank = jnp.sum(earlier * chosen, axis=1, keepdims=True)
    slot = jnp.where(rank < slots, where_to * slots + rank, -1.0)
    spots = lax.broadcasted_iota(jnp.int32, (pairs, TILE), 1).astype(F32)
    layout[...] = jnp.where(spots == slot, 1.0, 0.0).astype(BF16)

    crowded = jnp.where(jnp.max(rank, axis=0, keepdims=True) >= slots, 4.0, 0.0)
    filled = dot(layout[...], jnp.ones((pairs, 128), BF16), 0, 0)[:block_rows]
    lane_block = lax.broadcasted_iota(jnp.int32, (block_rows, 128), 1)
    row_block = lax.broadcasted_iota(jnp.int32, (block_rows, 128), 0)
    mark = 2.0 - 2.0 * filled
    if slots < MOST:
        mark += jnp.where(lax.rem(row_block, slots) == 0, crowded, 0.0)
    mark = jnp.where(lane_block == 0, mark, 0.0)

    def arrived(kind, k):
        return copy(
            pack.at[kind, chunk(k)],
            held.at[kind, chunk(k)],
            sa.at[kind],
            ra.at[kind, k],
            peer(k),
        )

    def gathered(kind, side, k):
        return copy(
            held.at[kind, chunk(k)],
            held.at[kind, chunk(k, PREV if side == 0 else NEXT)],
            sg.at[kind, side],
            rg.at[kind, k] if k % 2 == side else rh.at[kind, side],
            neighbour(kind, side),
        )

    def passed(kind, k):
        side = k % 2
        return copy(
            held.at[kind, chunk(k, PREV if side == 0 else NEXT)],
            held.at[kind, chunk(k, FAR)],
            sl.at[kind],
            rl.at[kind],
            neighbour(kind, side),
        )

    def send(kind, k):
        copy(
            pack.at[kind, chunk(k)],
            held.at[kind, chunk(facing(k))],
            sa.at[kind],
            ra.at[kind, facing(k)],
            peer(k),
        ).start()

    for kind in range(2):
        loads[2 * kind + 2].wait()
        loads[2 * kind + 3].wait()
        raw = dot(feats[kind], head[kind], 1, 0)
        scale_back = lax.rsqrt(jnp.sum(raw * raw, axis=1, keepdims=True) + EPS)
        unit[kind] = raw * scale_back
        factor[kind] = jnp.broadcast_to(scale_back, (pairs, 128))
        rows = dot(layout[...], unit[kind].astype(BF16), 0, 0)[:block_rows]
        first = (rows[:, :128] + mark).reshape(block, 8, 128)
        pack[kind, :, :, :128] = first.astype(BF16)
        pack[kind, :, :, 128:] = rows[:, 128:].reshape(block, 8, width - 128).astype(BF16)
        held[kind, :groups] = pack[kind, :groups]
        if kind == 0:
            pl.semaphore_wait(barrier, PEERS - 1 + 4)
        for k in ARRIVALS[:SOON]:
            send(kind, k)
        for side in range(2):
            gathered(kind, side, 0).start()
    for k in ARRIVALS[SOON:]:
        for kind in range(2):
            send(kind, k)

    def take(kind, k):
        arrived(kind, k).wait_recv()
        for side in range(2):
            gathered(kind, side, k).start()

    def pass_on(kind, k):
        gathered(kind, k % 2, k).wait_recv()
        passed(kind, k).start()

    takes = [(kind, k) for k in ARRIVALS for kind in range(2)]
    passes = [(kind, k) for k in (0,) + ARRIVALS for kind in range(2)]
    for n, one in enumerate(takes):
        take(*one)
        if n >= LAG:
            pass_on(*passes[n - LAG])
    for one in passes[len(takes) - LAG :]:
        pass_on(*one)

    for kind in range(2):
        for side in range(2):
            done(held.at[kind, pl.ds(0, block // 2)], rh.at[kind, side])

    loads[6].wait()
    loads[7].wait()
    scale_t = jnp.exp(scale[...])
    shift = bias[...]
    first_lane = jnp.where(lax.broadcasted_iota(jnp.int32, (8, 128), 1) == 0, 1.0, 0.0)
    losses[...] = jnp.zeros_like(losses)

    def tile_of(i, j, with_own):
        span = TILE // 8
        images = held[0, pl.ds(i * span, span)].reshape(TILE, width)
        texts = held[1, pl.ds(j * span, span)].reshape(TILE, width)
        sims = dot(images, texts, 1, 1)
        text_first = dot(first_lane.astype(BF16), texts[:, :128], 1, 1)[0:1]
        base = jnp.where(text_first < 1.5, shift * LOG2E, -1e5)
        powers = sims * (scale_t * LOG2E) + base
        if with_own:
            row = lax.broadcasted_iota(jnp.int32, (TILE, TILE), 0)
            same = row == lax.broadcasted_iota(jnp.int32, (TILE, TILE), 1)
            same = jnp.logical_and(same, row < block_rows)
            same = jnp.logical_and(same, powers > -5e4)
            powers = jnp.where(same, -powers, powers)
        odds = jnp.exp2(powers)
        whole = 1.0 + odds
        inverse = 1.0 / whole
        terms = jnp.log(whole) + (odds - (whole - 1.0)) * inverse
        rows = pl.ds(i * TILE, TILE)
        columns = pl.ds(j * TILE, TILE)
        losses[rows] += terms[:, :128] + terms[:, 128:]
        weights = odds * inverse * jnp.where(images[:, 0:1].astype(F32) < 1.5, scale_t, 0.0)
        if with_own:
            weights = jnp.where(same, -weights, weights)
        coef[rows, columns] = weights.astype(BF16)
        turned[columns, rows] = jnp.transpose(weights).astype(BF16)

    tile_of(0, 0, True)

    for t in range(1, early * early):
        tile_of(t // early, t % early, False)

    for kind in range(2):
        done(held.at[kind, pl.ds(0, block)], rl.at[kind])

    for t in range(early):
        tile_of(t, early, False)
    for t in range(early + 1):
        tile_of(early, t, False)

    alarm = None
    if slots < MOST:
        starts = jnp.zeros((8, 128), F32)
        for kind in range(2):
            starts = jnp.maximum(starts, jnp.max(held[kind, :, :, :128].astype(F32), axis=0))
        starts = jnp.where(lax.broadcasted_iota(jnp.int32, (8, 128), 1) == 0, starts, 0.0)
        starts = jnp.max(jnp.max(starts, axis=1, keepdims=True), axis=0, keepdims=True)
        alarm = jnp.where(starts > 2.5, 1.0, 0.0)
    else:
        alarm = jnp.zeros((1, 1), F32)

    def terms_of(kind, start, size):
        weights = coef if kind == 0 else turned

        for q in range(width // TILE):
            lanes = pl.ds(q * TILE, TILE)
            others = held[1 - kind, :, :, lanes].reshape(RING * block_rows, TILE)
            rows = pl.ds(start * block_rows, size * block_rows)
            part[kind, rows, lanes] = dot(weights[rows], others, 1, 0)

        rows = pl.ds(start * block_rows, size * block_rows)
        top = jnp.max(jnp.abs(part[kind, rows]), axis=1, keepdims=True)
        tops[kind, rows] = jnp.broadcast_to(top, (size * block_rows, 128))

    def at(n, k):
        return pl.ds(n * block_rows + k * slots, slots)

    total = jnp.sum(losses[...], axis=1, keepdims=True)
    losses[...] = jnp.broadcast_to(total, losses.shape)

    def mine(kind, n, k):
        rows = at(n, k)
        values, top = part[kind, rows], tops[kind, rows]
        if kind == 1:
            return values, top, None, None
        return values, top, losses[rows], jnp.broadcast_to(alarm, (slots, EXTRA))

    def both(one, other):
        sums = [a if b is None else a + b for a, b in zip(one[:3], other[:3])]
        return (*sums, None if one[3] is None else jnp.maximum(one[3], other[3]))

    parts = width // EXTRA * groups

    def store(kind, n, k, terms):
        steps, extra = encode(*terms)
        for l, step in enumerate(steps):
            step = step.reshape(groups, 8, EXTRA).astype(jnp.int32)
            away[kind, n, k, l * groups : (l + 1) * groups] = step.astype(jnp.int16)
        away[kind, n, k, parts] = extra.astype(jnp.int32).astype(jnp.int16)

    def load(ref, kind):
        coded = ref[...].astype(F32)
        extra = coded[parts]

        def field(f):
            each = [extra[:, 8 * r + f : 8 * r + f + 1] for r in range(groups)]
            return jnp.concatenate([jnp.broadcast_to(e, (8, EXTRA)) for e in each], axis=0)

        top = jnp.exp2(0.125 * field(0))
        step = top * (1.0 / LEVELS)
        values = [
            coded[l : l + groups].reshape(slots, EXTRA) * step for l in range(0, parts, groups)
        ]
        values = jnp.concatenate(values, axis=1)
        if kind == 1:
            return values, top, None, None
        return values, top, loss_from(field(1), field(2), field(3)), field(4)

    def first(kind, k):
        return copy(
            away.at[kind, FAR, k],
            far.at[k, kind],
            s1.at[kind],
            r1.at[k],
            neighbour(kind, k % 2),
        )

    def second(kind, side, k):
        return copy(
            away.at[kind, NEXT if side == 0 else PREV, k],
            near.at[k, kind, side],
            s2.at[kind, side],
            r2.at[k],
            neighbour(kind, side),
        )

    def returned(kind, k):
        return copy(
            away.at[kind, OWN, k],
            back.at[kind, k],
            sb.at[kind],
            rb.at[kind],
            peer(k),
        )

    def plain(k):
        return PREV if k % 2 == 0 else NEXT

    def mixed(k):
        return NEXT if k % 2 == 0 else PREV

    couples = ((7, 6), (5, 4), (3, 2), (1, 0))
    order = tuple(k for couple in couples for k in couple)
    for kind in range(2):
        terms_of(kind, FAR, 1)
        for some in (order[:2], order[2:]):
            for k in some:
                store(kind, FAR, k, mine(kind, FAR, k))
            for k in some[:4]:
                first(kind, k).start()

    for kind in range(2):
        terms_of(kind, NEXT, 2)
        for k in order:
            store(kind, plain(k), k, mine(kind, plain(k), k))
        for k in order[:2]:
            second(kind, 1 - k % 2, k).start()

    def send_on(couple):
        for k in couple:
            done(far.at[k], r1.at[k])
        for k in couple:
            for kind in range(2):
                more = load(far.at[k, kind], kind)
                store(kind, mixed(k), k, both(mine(kind, mixed(k), k), more))
        for k in couple:
            for kind in range(2):
                second(kind, k % 2, k).start()

    def send_back(k):
        done(near.at[k], r2.at[k])
        for kind in range(2):
            terms = mine(kind, OWN, k)
            for side in range(2):
                terms = both(terms, load(near.at[k, kind, side], kind))
            store(kind, OWN, k, terms)
        for kind in range(2):
            if k == 0:
                back[kind, 0] = away[kind, OWN, 0]
            else:
                copy(
                    away.at[kind, OWN, k],
                    back.at[kind, facing(k)],
                    sb.at[kind],
                    rb.at[kind],
                    peer(k),
                ).start()

    for n, couple in enumerate(couples):
        send_on(couple)
        if n == 0:
            for kind in range(2):
                for k in order[6:]:
                    first(kind, k).start()
        if n + 1 < len(couples):
            for kind in range(2):
                for k in couples[n + 1]:
                    second(kind, 1 - k % 2, k).start()
        if n == 0:
            for kind in range(2):
                terms_of(kind, OWN, 1)
        else:
            for k in couples[n - 1]:
                send_back(k)
    for k in couples[-1]:
        send_back(k)

    for kind, out in ((0, out_img), (1, out_txt)):
        done(back.at[kind, pl.ds(1, PEERS - 1)], rb.at[kind])
        coded = back[kind].astype(jnp.int32)
        extra = coded[:, parts].reshape(PEERS * 8, EXTRA)
        extras = [extra] + [pltpu.roll(extra, EXTRA - 8 * r, 1) for r in range(1, groups)]
        extras = [e.reshape(PEERS, 1, 8, EXTRA) for e in extras]
        lanes = [
            coded[:, l : l + groups].reshape(block_rows, EXTRA) for l in range(0, parts, groups)
        ]
        lanes.append(jnp.concatenate(extras, axis=1).reshape(block_rows, EXTRA))
        steps = jnp.concatenate(lanes, axis=1)
        high = lax.shift_right_arithmetic(steps, 8)
        low = steps - lax.shift_left(high, 8)
        pick = layout[:, :block_rows]
        high = dot(pick, high.astype(F32).astype(BF16), 1, 0)
        low = dot(pick, low.astype(F32).astype(BF16), 1, 0)
        own = high * 256.0 + low
        fields = [own[:, width + f : width + f + 1] for f in range(4)]
        grad = own[:, :width] * (jnp.exp2(0.125 * fields[0]) * (1.0 / LEVELS))
        if kind == 0:
            loss = loss_from(*fields[1:])
            loss = jnp.broadcast_to(loss * (1.0 / (RING * RING * pairs)), (pairs, pairs))
            out_loss[...] = jnp.transpose(loss)[0:1]
            out_alarm[0] = jnp.max(steps[:, width + 4 : width + 5])
        along = jnp.sum(unit[kind] * grad, axis=1, keepdims=True)
        out[...] = ((grad - unit[kind] * along) * factor[kind][:, 0:1]).astype(BF16)

    for kind in range(2):
        done(pack.at[kind, pl.ds(groups, block - groups)], sa.at[kind])
        done(held.at[kind, pl.ds(0, block)], sl.at[kind])
        done(away.at[kind, FAR], s1.at[kind])
        done(away.at[kind, OWN, pl.ds(1, PEERS - 1)], sb.at[kind])
        for side in range(2):
            done(held.at[kind, pl.ds(0, block)], sg.at[kind, side])
            done(away.at[kind, FAR], s2.at[kind, side])


def routed(slots, scale, bias, img_feats, txt_feats, img_head, txt_head, ids, placement):
    pairs, width = img_feats.shape[0], img_head.shape[1]
    deep = img_feats.shape[1]
    parts = width // EXTRA * (slots // 8) + 1
    block = PEERS * slots // 8
    rows = RING * PEERS * slots
    dma, vmem = pltpu.SemaphoreType.DMA, pl.BlockSpec(memory_space=pltpu.VMEM)
    smem, away = pl.BlockSpec(memory_space=pltpu.SMEM), pl.BlockSpec(memory_space=pl.ANY)
    return pl.pallas_call(
        functools.partial(kernel, slots),
        out_shape=(
            jax.ShapeDtypeStruct((pairs, width), BF16),
            jax.ShapeDtypeStruct((pairs, width), BF16),
            jax.ShapeDtypeStruct((1, pairs), F32),
            jax.ShapeDtypeStruct((1,), jnp.int32),
        ),
        in_specs=[away] * 8,
        out_specs=(vmem, vmem, vmem, smem),
        scratch_shapes=[
            pltpu.VMEM((1, 1), F32),
            pltpu.VMEM((1, 1), F32),
            pltpu.VMEM((1, pairs), jnp.int32),
            pltpu.VMEM((1, pairs), jnp.int32),
            pltpu.VMEM((2, pairs, deep), BF16),
            pltpu.VMEM((2, deep, width), BF16),
            pltpu.VMEM((pairs, TILE), BF16),
            pltpu.VMEM((2, pairs, width), F32),
            pltpu.VMEM((2, pairs, 128), F32),
            pltpu.VMEM((2, block, 8, width), BF16),
            pltpu.VMEM((2, RING * block, 8, width), BF16),
            pltpu.VMEM((rows, rows), BF16),
            pltpu.VMEM((rows, rows), BF16),
            pltpu.VMEM((rows, 128), F32),
            pltpu.VMEM((2, rows, width), F32),
            pltpu.VMEM((2, rows, 128), F32),
            pltpu.VMEM((2, RING, PEERS, parts, 8, EXTRA), jnp.int16),
            pltpu.VMEM((PEERS, 2, 2, parts, 8, EXTRA), jnp.int16),
            pltpu.VMEM((PEERS, 2, parts, 8, EXTRA), jnp.int16),
            pltpu.VMEM((2, PEERS, parts, 8, EXTRA), jnp.int16),
            dma((8,)),
            dma((2,)),
            dma((2, PEERS)),
            dma((2, 2)),
            dma((2, PEERS)),
            dma((2, 2)),
            dma((2,)),
            dma((2,)),
            dma((2,)),
            dma((PEERS,)),
            dma((2, 2)),
            dma((PEERS,)),
            dma((2,)),
            dma((2,)),
        ],
        compiler_params=pltpu.CompilerParams(
            collective_id=slots // 8,
            has_side_effects=True,
            vmem_limit_bytes=(48 if slots == MOST else 40) * 1024 * 1024,
        ),
    )(scale, bias, img_feats, txt_feats, img_head, txt_head, ids, placement)


def final_kernel(
    img_local, txt_local, img_head, txt_head, loss, out_img, out_txt, out_loss, done, sems
):
    copies = []
    for kind, (local, head, out) in enumerate(
        ((img_local, img_head, out_img), (txt_local, txt_head, out_txt))
    ):
        done[kind] = dot(local[...], head[...], 1, 1)
        copies.append(pltpu.make_async_copy(done.at[kind], out, sems.at[kind]))
        copies[-1].start()
    out_loss[...] = loss[...]
    for copy in copies:
        copy.wait()


def final(img_local, txt_local, img_head, txt_head, loss):
    pairs, width = img_local.shape
    deep = img_head.shape[0]
    vmem, away = pl.BlockSpec(memory_space=pltpu.VMEM), pl.BlockSpec(memory_space=pl.ANY)
    return pl.pallas_call(
        final_kernel,
        out_shape=(
            jax.ShapeDtypeStruct((pairs, deep), F32),
            jax.ShapeDtypeStruct((pairs, deep), F32),
            jax.ShapeDtypeStruct((1, pairs), F32),
        ),
        in_specs=[vmem] * 5,
        out_specs=(away, away, vmem),
        scratch_shapes=[pltpu.VMEM((2, pairs, deep), F32), pltpu.SemaphoreType.DMA((2,))],
        compiler_params=pltpu.CompilerParams(vmem_limit_bytes=12 * 1024 * 1024),
    )(img_local, txt_local, img_head, txt_head, loss)


FAST = 24


def body(img_feats, txt_feats, img_head, txt_head, cluster_ids, placement, log_scale, bias):
    arguments = (log_scale.reshape(1, 1), bias.reshape(1, 1), img_feats, txt_feats, img_head, txt_head)
    arguments += (cluster_ids.reshape(1, -1), placement.reshape(1, -1))
    img_local, txt_local, loss, alarm = routed(FAST, *arguments)

    def ample():
        img_local, txt_local, loss, _ = routed(MOST, *arguments)
        return final(img_local, txt_local, img_head, txt_head, loss)

    def kept():
        return final(img_local, txt_local, img_head, txt_head, loss)

    img, txt, loss = lax.cond(alarm[0] > 0, ample, kept)
    return img, txt, loss.reshape(-1)


def solution(mesh):
    placed = (
        P(("grp", "blk"), None),
        P(("grp", "blk"), None),
        P(),
        P(),
        P(("grp", "blk"), None),
        P(),
        P(),
        P(),
    )
    return jax.shard_map(
        body,
        mesh=mesh,
        in_specs=placed,
        out_specs=(P(("grp", "blk"), None), P(("grp", "blk"), None), P(("grp", "blk"))),
        check_vma=False,
    )
```

```python
import functools

import jax
import jax.numpy as jnp
from jax import lax
from jax.experimental import pallas as pl
from jax.experimental.pallas import tpu as pltpu
from jax.sharding import PartitionSpec as P

EPS = 1e-06
CORES = 2
RING = 4
PEERS = 8
MOST = 32
TILE = 256
EXTRA = 128
LEVELS = 32000.0
AROUND = (0, 1, 3, 2)
ARRIVALS = (1, 2, 4, 3, 5, 6, 7)
SOON = 3
LAG = 6
FACING = (0, 2, 1, 3)
OWN, NEXT, PREV, FAR = range(4)
MESH = pl.DeviceIdType.MESH
F32 = jnp.float32
BF16 = jnp.bfloat16
LOG2E = 1.4426950408889634


def dot(a, b, da, db):
    return lax.dot_general(a, b, (((da,), (db,)), ((), ())), preferred_element_type=F32)


def encode(values, top, loss, alarm):
    grade = jnp.ceil(8.0 * jnp.log2(jnp.maximum(top, 1e-30)))
    scale = LEVELS * jnp.exp2(-0.125 * grade)
    steps = [jnp.round(values[:, n : n + EXTRA] * scale) for n in range(0, values.shape[1], EXTRA)]
    fields = [grade]
    if loss is not None:
        loss_grade = jnp.ceil(8.0 * jnp.log2(jnp.maximum(loss, 1e-30)))
        scaled = loss * (LEVELS * jnp.exp2(-0.125 * loss_grade))
        high = jnp.round(scaled)
        low = jnp.round((scaled - high) * LEVELS)
        fields += [loss_grade, high, low, alarm]
    lane = lax.broadcasted_iota(jnp.int32, (8, EXTRA), 1)
    extra = jnp.zeros((8, EXTRA), F32)
    for r in range(values.shape[0] // 8):
        for f, field in enumerate(fields):
            extra = jnp.where(lane == 8 * r + f, field[8 * r : 8 * r + 8], extra)
    return steps, extra


def loss_from(loss_grade, high, low):
    scale = jnp.exp2(0.125 * loss_grade) * (1.0 / LEVELS)
    return (high + low * (1.0 / LEVELS)) * scale


def kernel(
    slots,
    scale_in,
    bias_in,
    img_feats,
    txt_feats,
    img_head,
    txt_head,
    ids_in,
    placement_in,
    out_img,
    out_txt,
    out_loss,
    out_alarm,
    scale,
    bias,
    ids,
    placement,
    feats,
    head,
    layout,
    unit,
    factor,
    pack,
    held,
    coef,
    turned,
    losses,
    part,
    tops,
    away,
    near,
    far,
    back,
    si,
    sa,
    ra,
    sg,
    rg,
    rh,
    sl,
    rl,
    s1,
    r1,
    s2,
    r2,
    sb,
    rb,
):
    width = img_head.shape[1]
    pairs = img_feats.shape[0]
    groups = slots // 8
    block = PEERS * groups
    block_rows = PEERS * slots
    early = 3 * block_rows // TILE
    g = lax.axis_index("grp")
    b = lax.axis_index("blk")
    x, core = lax.div(g, CORES), lax.rem(g, CORES)
    y, z = lax.div(b, RING), lax.rem(b, RING)

    def peer(k):
        to_x = lax.rem(x + AROUND[k // CORES], RING)
        return (to_x * CORES + lax.rem(core + k % CORES, CORES), b)

    def facing(k):
        return FACING[k // CORES] * CORES + k % CORES

    def neighbour(kind, side):
        step = 1 if side == 0 else RING - 1
        if kind == 0:
            return (g, y * RING + lax.rem(z + step, RING))
        return (g, lax.rem(y + step, RING) * RING + z)

    def copy(src, dst, send, recv, device):
        return pltpu.make_async_remote_copy(
            src_ref=src,
            dst_ref=dst,
            send_sem=send,
            recv_sem=recv,
            device_id=device,
            device_id_type=MESH,
        )

    def done(ref, sem):
        pltpu.make_async_copy(ref, ref, sem).wait()

    def chunk(k, at=0):
        return pl.ds(at * block + k * groups, groups)

    loads = []
    for n, (src, dst) in enumerate(
        (
            (ids_in, ids),
            (placement_in, placement),
            (img_feats, feats.at[0]),
            (img_head, head.at[0]),
            (txt_feats, feats.at[1]),
            (txt_head, head.at[1]),
            (scale_in, scale),
            (bias_in, bias),
        )
    ):
        loads.append(pltpu.make_async_copy(src, dst, si.at[n]))
        loads[-1].start()

    barrier = pltpu.get_barrier_semaphore()
    for k in range(1, PEERS):
        pl.semaphore_signal(barrier, inc=1, device_id=peer(k), device_id_type=MESH)
    for kind in range(2):
        for side in range(2):
            pl.semaphore_signal(
                barrier, inc=1, device_id=neighbour(kind, side), device_id_type=MESH
            )

    loads[0].wait()
    loads[1].wait()
    lane = lax.broadcasted_iota(jnp.int32, (pairs, 128), 1)
    row = lax.broadcasted_iota(jnp.int32, (pairs, 128), 0)
    lane_f = lane.astype(F32)
    place = placement[...].astype(F32)
    named = jnp.transpose(jnp.broadcast_to(ids[...].astype(F32), (pairs, pairs)))
    target = jnp.sum(jnp.where(named == lane_f, place, 0.0), axis=1, keepdims=True)
    team = jnp.floor(target * (1.0 / (RING * RING)))
    team_x = jnp.floor(team * (1.0 / CORES))
    dx = team_x - x.astype(F32)
    dx = jnp.where(dx < 0, dx + RING, dx)
    dx = jnp.where(dx == 2, 3.0, jnp.where(dx == 3, 2.0, dx))
    dc = team - CORES * team_x - core.astype(F32)
    where_to = CORES * dx + jnp.where(dc < 0, dc + CORES, dc)
    chosen = jnp.where(where_to == lane_f, 1.0, 0.0)
    before = jnp.where(row > lane, 1.0, 0.0).astype(BF16)
    earlier = dot(before, chosen.astype(BF16), 1, 0)
    rank = jnp.sum(earlier * chosen, axis=1, keepdims=True)
    slot = jnp.where(rank < slots, where_to * slots + rank, -1.0)
    spots = lax.broadcasted_iota(jnp.int32, (pairs, TILE), 1).astype(F32)
    layout[...] = jnp.where(spots == slot, 1.0, 0.0).astype(BF16)

    crowded = jnp.where(jnp.max(rank, axis=0, keepdims=True) >= slots, 4.0, 0.0)
    filled = dot(layout[...], jnp.ones((pairs, 128), BF16), 0, 0)[:block_rows]
    lane_block = lax.broadcasted_iota(jnp.int32, (block_rows, 128), 1)
    row_block = lax.broadcasted_iota(jnp.int32, (block_rows, 128), 0)
    mark = 2.0 - 2.0 * filled
    if slots < MOST:
        mark += jnp.where(lax.rem(row_block, slots) == 0, crowded, 0.0)
    mark = jnp.where(lane_block == 0, mark, 0.0)

    def arrived(kind, k):
        return copy(
            pack.at[kind, chunk(k)],
            held.at[kind, chunk(k)],
            sa.at[kind],
            ra.at[kind, k],
            peer(k),
        )

    def gathered(kind, side, k):
        return copy(
            held.at[kind, chunk(k)],
            held.at[kind, chunk(k, PREV if side == 0 else NEXT)],
            sg.at[kind, side],
            rg.at[kind, k] if k % 2 == side else rh.at[kind, side],
            neighbour(kind, side),
        )

    def passed(kind, k):
        side = k % 2
        return copy(
            held.at[kind, chunk(k, PREV if side == 0 else NEXT)],
            held.at[kind, chunk(k, FAR)],
            sl.at[kind],
            rl.at[kind],
            neighbour(kind, side),
        )

    def send(kind, k):
        copy(
            pack.at[kind, chunk(k)],
            held.at[kind, chunk(facing(k))],
            sa.at[kind],
            ra.at[kind, facing(k)],
            peer(k),
        ).start()

    for kind in range(2):
        loads[2 * kind + 2].wait()
        loads[2 * kind + 3].wait()
        raw = dot(feats[kind], head[kind], 1, 0)
        scale_back = lax.rsqrt(jnp.sum(raw * raw, axis=1, keepdims=True) + EPS)
        unit[kind] = raw * scale_back
        factor[kind] = jnp.broadcast_to(scale_back, (pairs, 128))
        rows = dot(layout[...], unit[kind].astype(BF16), 0, 0)[:block_rows]
        first = (rows[:, :128] + mark).reshape(block, 8, 128)
        pack[kind, :, :, :128] = first.astype(BF16)
        pack[kind, :, :, 128:] = rows[:, 128:].reshape(block, 8, width - 128).astype(BF16)
        held[kind, :groups] = pack[kind, :groups]
        if kind == 0:
            pl.semaphore_wait(barrier, PEERS - 1 + 4)
        for k in ARRIVALS[:SOON]:
            send(kind, k)
        for side in range(2):
            gathered(kind, side, 0).start()
    for k in ARRIVALS[SOON:]:
        for kind in range(2):
            send(kind, k)

    def take(kind, k):
        arrived(kind, k).wait_recv()
        for side in range(2):
            gathered(kind, side, k).start()

    def pass_on(kind, k):
        gathered(kind, k % 2, k).wait_recv()
        passed(kind, k).start()

    takes = [(kind, k) for k in ARRIVALS for kind in range(2)]
    passes = [(kind, k) for k in (0,) + ARRIVALS for kind in range(2)]
    for n, one in enumerate(takes):
        take(*one)
        if n >= LAG:
            pass_on(*passes[n - LAG])
    for one in passes[len(takes) - LAG :]:
        pass_on(*one)

    for kind in range(2):
        for side in range(2):
            done(held.at[kind, pl.ds(0, block // 2)], rh.at[kind, side])

    loads[6].wait()
    loads[7].wait()
    scale_t = jnp.exp(scale[...])
    shift = bias[...]
    first_lane = jnp.where(lax.broadcasted_iota(jnp.int32, (8, 128), 1) == 0, 1.0, 0.0)
    losses[...] = jnp.zeros_like(losses)

    def tile_of(i, j, with_own):
        span = TILE // 8
        images = held[0, pl.ds(i * span, span)].reshape(TILE, width)
        texts = held[1, pl.ds(j * span, span)].reshape(TILE, width)
        sims = dot(images, texts, 1, 1)
        text_first = dot(first_lane.astype(BF16), texts[:, :128], 1, 1)[0:1]
        base = jnp.where(text_first < 1.5, shift * LOG2E, -1e5)
        powers = sims * (scale_t * LOG2E) + base
        if with_own:
            row = lax.broadcasted_iota(jnp.int32, (TILE, TILE), 0)
            same = row == lax.broadcasted_iota(jnp.int32, (TILE, TILE), 1)
            same = jnp.logical_and(same, row < block_rows)
            same = jnp.logical_and(same, powers > -5e4)
            powers = jnp.where(same, -powers, powers)
        odds = jnp.exp2(powers)
        whole = 1.0 + odds
        inverse = 1.0 / whole
        terms = jnp.log(whole) + (odds - (whole - 1.0)) * inverse
        rows = pl.ds(i * TILE, TILE)
        columns = pl.ds(j * TILE, TILE)
        losses[rows] += terms[:, :128] + terms[:, 128:]
        weights = odds * inverse * jnp.where(images[:, 0:1].astype(F32) < 1.5, scale_t, 0.0)
        if with_own:
            weights = jnp.where(same, -weights, weights)
        coef[rows, columns] = weights.astype(BF16)
        turned[columns, rows] = jnp.transpose(weights).astype(BF16)

    tile_of(0, 0, True)

    for t in range(1, early * early):
        tile_of(t // early, t % early, False)

    for kind in range(2):
        done(held.at[kind, pl.ds(0, block)], rl.at[kind])

    for t in range(early):
        tile_of(t, early, False)
    for t in range(early + 1):
        tile_of(early, t, False)

    alarm = None
    if slots < MOST:
        starts = jnp.zeros((8, 128), F32)
        for kind in range(2):
            starts = jnp.maximum(starts, jnp.max(held[kind, :, :, :128].astype(F32), axis=0))
        starts = jnp.where(lax.broadcasted_iota(jnp.int32, (8, 128), 1) == 0, starts, 0.0)
        starts = jnp.max(jnp.max(starts, axis=1, keepdims=True), axis=0, keepdims=True)
        alarm = jnp.where(starts > 2.5, 1.0, 0.0)
    else:
        alarm = jnp.zeros((1, 1), F32)

    def terms_of(kind, start, size):
        weights = coef if kind == 0 else turned

        for q in range(width // TILE):
            lanes = pl.ds(q * TILE, TILE)
            others = held[1 - kind, :, :, lanes].reshape(RING * block_rows, TILE)
            rows = pl.ds(start * block_rows, size * block_rows)
            part[kind, rows, lanes] = dot(weights[rows], others, 1, 0)

        rows = pl.ds(start * block_rows, size * block_rows)
        top = jnp.max(jnp.abs(part[kind, rows]), axis=1, keepdims=True)
        tops[kind, rows] = jnp.broadcast_to(top, (size * block_rows, 128))

    def at(n, k):
        return pl.ds(n * block_rows + k * slots, slots)

    total = jnp.sum(losses[...], axis=1, keepdims=True)
    losses[...] = jnp.broadcast_to(total, losses.shape)

    def mine(kind, n, k):
        rows = at(n, k)
        values, top = part[kind, rows], tops[kind, rows]
        if kind == 1:
            return values, top, None, None
        return values, top, losses[rows], jnp.broadcast_to(alarm, (slots, EXTRA))

    def both(one, other):
        sums = [a if b is None else a + b for a, b in zip(one[:3], other[:3])]
        return (*sums, None if one[3] is None else jnp.maximum(one[3], other[3]))

    parts = width // EXTRA * groups

    def store(kind, n, k, terms):
        steps, extra = encode(*terms)
        for l, step in enumerate(steps):
            step = step.reshape(groups, 8, EXTRA).astype(jnp.int32)
            away[kind, n, k, l * groups : (l + 1) * groups] = step.astype(jnp.int16)
        away[kind, n, k, parts] = extra.astype(jnp.int32).astype(jnp.int16)

    def load(ref, kind):
        coded = ref[...].astype(F32)
        extra = coded[parts]

        def field(f):
            each = [extra[:, 8 * r + f : 8 * r + f + 1] for r in range(groups)]
            return jnp.concatenate([jnp.broadcast_to(e, (8, EXTRA)) for e in each], axis=0)

        top = jnp.exp2(0.125 * field(0))
        step = top * (1.0 / LEVELS)
        values = [
            coded[l : l + groups].reshape(slots, EXTRA) * step for l in range(0, parts, groups)
        ]
        values = jnp.concatenate(values, axis=1)
        if kind == 1:
            return values, top, None, None
        return values, top, loss_from(field(1), field(2), field(3)), field(4)

    def first(kind, k):
        return copy(
            away.at[kind, FAR, k],
            far.at[k, kind],
            s1.at[kind],
            r1.at[k],
            neighbour(kind, k % 2),
        )

    def second(kind, side, k):
        return copy(
            away.at[kind, NEXT if side == 0 else PREV, k],
            near.at[k, kind, side],
            s2.at[kind, side],
            r2.at[k],
            neighbour(kind, side),
        )

    def returned(kind, k):
        return copy(
            away.at[kind, OWN, k],
            back.at[kind, k],
            sb.at[kind],
            rb.at[kind],
            peer(k),
        )

    def plain(k):
        return PREV if k % 2 == 0 else NEXT

    def mixed(k):
        return NEXT if k % 2 == 0 else PREV

    couples = ((7, 6), (5, 4), (3, 2), (1, 0))
    order = tuple(k for couple in couples for k in couple)
    for kind in range(2):
        terms_of(kind, FAR, 1)
        for some in (order[:2], order[2:]):
            for k in some:
                store(kind, FAR, k, mine(kind, FAR, k))
            for k in some[:4]:
                first(kind, k).start()

    for kind in range(2):
        terms_of(kind, NEXT, 2)
        for k in order:
            store(kind, plain(k), k, mine(kind, plain(k), k))
        for k in order[:2]:
            second(kind, 1 - k % 2, k).start()

    def send_on(couple):
        for k in couple:
            done(far.at[k], r1.at[k])
        for k in couple:
            for kind in range(2):
                more = load(far.at[k, kind], kind)
                store(kind, mixed(k), k, both(mine(kind, mixed(k), k), more))
        for k in couple:
            for kind in range(2):
                second(kind, k % 2, k).start()

    def send_back(k):
        done(near.at[k], r2.at[k])
        for kind in range(2):
            terms = mine(kind, OWN, k)
            for side in range(2):
                terms = both(terms, load(near.at[k, kind, side], kind))
            store(kind, OWN, k, terms)
        for kind in range(2):
            if k == 0:
                back[kind, 0] = away[kind, OWN, 0]
            else:
                copy(
                    away.at[kind, OWN, k],
                    back.at[kind, facing(k)],
                    sb.at[kind],
                    rb.at[kind],
                    peer(k),
                ).start()

    for n, couple in enumerate(couples):
        send_on(couple)
        if n == 0:
            for kind in range(2):
                for k in order[6:]:
                    first(kind, k).start()
        if n + 1 < len(couples):
            for kind in range(2):
                for k in couples[n + 1]:
                    second(kind, 1 - k % 2, k).start()
        if n == 0:
            for kind in range(2):
                terms_of(kind, OWN, 1)
        else:
            for k in couples[n - 1]:
                send_back(k)
    for k in couples[-1]:
        send_back(k)

    for kind, out in ((0, out_img), (1, out_txt)):
        done(back.at[kind, pl.ds(1, PEERS - 1)], rb.at[kind])
        coded = back[kind].astype(jnp.int32)
        extra = coded[:, parts].reshape(PEERS * 8, EXTRA)
        extras = [extra] + [pltpu.roll(extra, EXTRA - 8 * r, 1) for r in range(1, groups)]
        extras = [e.reshape(PEERS, 1, 8, EXTRA) for e in extras]
        lanes = [
            coded[:, l : l + groups].reshape(block_rows, EXTRA) for l in range(0, parts, groups)
        ]
        lanes.append(jnp.concatenate(extras, axis=1).reshape(block_rows, EXTRA))
        steps = jnp.concatenate(lanes, axis=1)
        high = lax.shift_right_arithmetic(steps, 8)
        low = steps - lax.shift_left(high, 8)
        pick = layout[:, :block_rows]
        high = dot(pick, high.astype(F32).astype(BF16), 1, 0)
        low = dot(pick, low.astype(F32).astype(BF16), 1, 0)
        own = high * 256.0 + low
        fields = [own[:, width + f : width + f + 1] for f in range(4)]
        grad = own[:, :width] * (jnp.exp2(0.125 * fields[0]) * (1.0 / LEVELS))
        if kind == 0:
            loss = loss_from(*fields[1:])
            loss = jnp.broadcast_to(loss * (1.0 / (RING * RING * pairs)), (pairs, pairs))
            out_loss[...] = jnp.transpose(loss)[0:1]
            out_alarm[0] = jnp.max(steps[:, width + 4 : width + 5])
        along = jnp.sum(unit[kind] * grad, axis=1, keepdims=True)
        out[...] = ((grad - unit[kind] * along) * factor[kind][:, 0:1]).astype(BF16)

    for kind in range(2):
        done(pack.at[kind, pl.ds(groups, block - groups)], sa.at[kind])
        done(held.at[kind, pl.ds(0, block)], sl.at[kind])
        done(away.at[kind, FAR], s1.at[kind])
        done(away.at[kind, OWN, pl.ds(1, PEERS - 1)], sb.at[kind])
        for side in range(2):
            done(held.at[kind, pl.ds(0, block)], sg.at[kind, side])
            done(away.at[kind, FAR], s2.at[kind, side])


def routed(slots, scale, bias, img_feats, txt_feats, img_head, txt_head, ids, placement):
    pairs, width = img_feats.shape[0], img_head.shape[1]
    deep = img_feats.shape[1]
    parts = width // EXTRA * (slots // 8) + 1
    block = PEERS * slots // 8
    rows = RING * PEERS * slots
    dma, vmem = pltpu.SemaphoreType.DMA, pl.BlockSpec(memory_space=pltpu.VMEM)
    smem, away = pl.BlockSpec(memory_space=pltpu.SMEM), pl.BlockSpec(memory_space=pl.ANY)
    return pl.pallas_call(
        functools.partial(kernel, slots),
        out_shape=(
            jax.ShapeDtypeStruct((pairs, width), BF16),
            jax.ShapeDtypeStruct((pairs, width), BF16),
            jax.ShapeDtypeStruct((1, pairs), F32),
            jax.ShapeDtypeStruct((1,), jnp.int32),
        ),
        in_specs=[away] * 8,
        out_specs=(vmem, vmem, vmem, smem),
        scratch_shapes=[
            pltpu.VMEM((1, 1), F32),
            pltpu.VMEM((1, 1), F32),
            pltpu.VMEM((1, pairs), jnp.int32),
            pltpu.VMEM((1, pairs), jnp.int32),
            pltpu.VMEM((2, pairs, deep), BF16),
            pltpu.VMEM((2, deep, width), BF16),
            pltpu.VMEM((pairs, TILE), BF16),
            pltpu.VMEM((2, pairs, width), F32),
            pltpu.VMEM((2, pairs, 128), F32),
            pltpu.VMEM((2, block, 8, width), BF16),
            pltpu.VMEM((2, RING * block, 8, width), BF16),
            pltpu.VMEM((rows, rows), BF16),
            pltpu.VMEM((rows, rows), BF16),
            pltpu.VMEM((rows, 128), F32),
            pltpu.VMEM((2, rows, width), F32),
            pltpu.VMEM((2, rows, 128), F32),
            pltpu.VMEM((2, RING, PEERS, parts, 8, EXTRA), jnp.int16),
            pltpu.VMEM((PEERS, 2, 2, parts, 8, EXTRA), jnp.int16),
            pltpu.VMEM((PEERS, 2, parts, 8, EXTRA), jnp.int16),
            pltpu.VMEM((2, PEERS, parts, 8, EXTRA), jnp.int16),
            dma((8,)),
            dma((2,)),
            dma((2, PEERS)),
            dma((2, 2)),
            dma((2, PEERS)),
            dma((2, 2)),
            dma((2,)),
            dma((2,)),
            dma((2,)),
            dma((PEERS,)),
            dma((2, 2)),
            dma((PEERS,)),
            dma((2,)),
            dma((2,)),
        ],
        compiler_params=pltpu.CompilerParams(
            collective_id=slots // 8,
            has_side_effects=True,
            vmem_limit_bytes=(48 if slots == MOST else 40) * 1024 * 1024,
        ),
    )(scale, bias, img_feats, txt_feats, img_head, txt_head, ids, placement)


def final_kernel(
    img_local, txt_local, img_head, txt_head, loss, out_img, out_txt, out_loss, done, sems
):
    copies = []
    for kind, (local, head, out) in enumerate(
        ((img_local, img_head, out_img), (txt_local, txt_head, out_txt))
    ):
        half = head.shape[0] // 2
        for n in range(2):
            some = pl.ds(n * half, half)
            done[kind, :, some] = dot(local[...], head[some], 1, 1)
            copies.append(
                pltpu.make_async_copy(done.at[kind, :, some], out.at[:, some], sems.at[kind, n])
            )
            copies[-1].start()
    out_loss[...] = loss[...]
    for copy in copies:
        copy.wait()


def final(img_local, txt_local, img_head, txt_head, loss):
    pairs, width = img_local.shape
    deep = img_head.shape[0]
    vmem, away = pl.BlockSpec(memory_space=pltpu.VMEM), pl.BlockSpec(memory_space=pl.ANY)
    return pl.pallas_call(
        final_kernel,
        out_shape=(
            jax.ShapeDtypeStruct((pairs, deep), F32),
            jax.ShapeDtypeStruct((pairs, deep), F32),
            jax.ShapeDtypeStruct((1, pairs), F32),
        ),
        in_specs=[vmem] * 5,
        out_specs=(away, away, vmem),
        scratch_shapes=[pltpu.VMEM((2, pairs, deep), F32), pltpu.SemaphoreType.DMA((2, 2))],
        compiler_params=pltpu.CompilerParams(vmem_limit_bytes=12 * 1024 * 1024),
    )(img_local, txt_local, img_head, txt_head, loss)


FAST = 24


def body(img_feats, txt_feats, img_head, txt_head, cluster_ids, placement, log_scale, bias):
    arguments = (log_scale.reshape(1, 1), bias.reshape(1, 1), img_feats, txt_feats, img_head, txt_head)
    arguments += (cluster_ids.reshape(1, -1), placement.reshape(1, -1))
    img_local, txt_local, loss, alarm = routed(FAST, *arguments)

    def ample():
        img_local, txt_local, loss, _ = routed(MOST, *arguments)
        return final(img_local, txt_local, img_head, txt_head, loss)

    def kept():
        return final(img_local, txt_local, img_head, txt_head, loss)

    img, txt, loss = lax.cond(alarm[0] > 0, ample, kept)
    return img, txt, loss.reshape(-1)


def solution(mesh):
    placed = (
        P(("grp", "blk"), None),
        P(("grp", "blk"), None),
        P(),
        P(),
        P(("grp", "blk"), None),
        P(),
        P(),
        P(),
    )
    return jax.shard_map(
        body,
        mesh=mesh,
        in_specs=placed,
        out_specs=(P(("grp", "blk"), None), P(("grp", "blk"), None), P(("grp", "blk"))),
        check_vma=False,
    )
```
